512 devices in a mesh: slab: 8 (over z_lo, core), subj: 32 (over x, y), comp: 2 (over z_hi).
Axes of the slice: x: 4, y: 8, z: 8 (z_hi: 2, z_lo: 4; z = z_hi * 4 + z_lo), core: 2. Of those that a mesh axis runs over, the one named last changes fastest.
Arguments:
- scans: bfloat16 [14336, 8, 32, 128], P('subj', 'slab'), may hold values from -6 to 6
- maps: bfloat16 [256, 8, 32, 128], P('comp', 'slab'), may hold values from -4 to 4
- gram_old: float32 [256, 256], P('comp'), may hold values from -0.04 to 2, as said below
- stats_old: float32 [256, 8, 32, 128], P('comp', 'slab', 'subj'), may hold values from -6 to 6
- kept: int32 [32], P('subj'), may hold values from 224 to 448, as said below
Outputs:
- maps_new: bfloat16 [256, 8, 32, 128], P('comp', 'slab', 'subj')
- stats_new: float32 [256, 8, 32, 128], P('comp', 'slab', 'subj')
- gram_new: float32 [256, 256], P('comp')
- codes: float32 [14336, 256], P('subj', 'comp')
The draws below stay inside these ranges and needn't reach their ends.
Inputs may be any that keep to these rules, and one draw needn't show every extreme that they name: Subject s uses its volumes 0 to kept[s] - 1 in the statistics; some subject keeps all 448. `gram_old`: Symmetric, with a diagonal of 0.5 or more.
All inputs are finite; a program needn't handle non-finite values.
Results may differ from the reference program's by a relative error of at most 0.017.
Values may be sent and summed in bfloat16 or wider, within the bound.
No kernel may reach another device: no remote copies, remote signals or barrier semaphores. Data moves between devices by JAX's collectives and lax.ppermute only.
A program may use at most 64 MiB of HBM per device.

```python
import math
import jax
import jax.numpy as jnp
from jax import lax

COMPONENTS = 256
VOLUMES = 448
GRID_X = 128
ITERS = 12
SUBJECTS = 32
ROWS = 14336
GRID_Y = 32
GRID_Z = 8
VOXELS = 32768


def draw_gram_old(key, part):
    key = jax.random.fold_in(key, 1)
    first, second = jax.random.split(key)
    off_diag = jax.random.uniform(first, (COMPONENTS, COMPONENTS), jnp.float32, -0.04, 0.04)
    off_diag = (off_diag + off_diag.T) * 0.5
    diag = jax.random.uniform(second, (COMPONENTS,), jnp.float32, 0.5, 2.0)
    index = jnp.arange(COMPONENTS)
    on_diag = index[:, None] == index[None, :]
    return jnp.where(on_diag, diag[:, None] * jnp.ones((1, COMPONENTS), jnp.float32), off_diag)


def draw_kept(key, part):
    key = jax.random.fold_in(key, 2)
    first, second = jax.random.split(key)
    values = jax.random.randint(first, (SUBJECTS,), VOLUMES // 2, VOLUMES + 1, dtype=jnp.int32)
    chosen = jax.random.randint(second, (), 0, SUBJECTS, dtype=jnp.int32)
    return jnp.where(jnp.arange(SUBJECTS, dtype=jnp.int32) == chosen, VOLUMES, values).astype(jnp.int32)


def raised(result, own_key, source, target, shards_of, factor):
    def block_of(axis_at):
        return (jnp.arange(result.shape[axis_at]) // (result.shape[axis_at] // shards_of)).reshape((-1,) + (1,) * (result.ndim - 1 - axis_at))

    first = jax.random.permutation(own_key, shards_of)[block_of(target)]
    far = (block_of(target) + shards_of // 2) % shards_of
    return jnp.where((block_of(source) == first) | (block_of(source) == far), factor * result, result)


def shard_levels(own_key, dims, cuts, least, top_value):
    factor_of, own = 1.0, jax.random.fold_in(own_key, 6)
    for axis_at, shards_of in cuts:
        heights = jnp.exp(jax.random.uniform(jax.random.fold_in(own, axis_at), (shards_of,), jnp.float32, least / len(cuts), top_value / len(cuts)))
        factor_of = factor_of * jnp.repeat(heights, dims[axis_at] // shards_of).reshape([-1 if axis == axis_at else 1 for axis in range(len(dims))])
    return factor_of


def centred(key, shape, scale, bound, pieces=(), kind=jnp.bfloat16):
    drawn = jax.random.normal(key, shape, jnp.float32) * scale
    if len(pieces) > 0:
        drawn = shard_levels(key, shape, pieces, -0.22, 0.18) * drawn
    return jnp.clip(drawn, min=-bound, max=bound).astype(kind)


def gaussian_with(own_key, extent, spread, reach, cuts, heavy, kind=jnp.bfloat16):
    values = spread * jax.random.normal(own_key, extent, jnp.float32)
    if cuts:
        values = values * shard_levels(own_key, extent, cuts, -0.22, 0.18)
    return jnp.clip(raised(values, jax.random.fold_in(own_key, 3), *heavy), -reach, reach).astype(kind)


def setup_inputs(seed: int = 0) -> dict:
    streams_of = jax.random.split(jax.random.key(seed), 6)
    scans = gaussian_with(streams_of[0], (ROWS, GRID_Z, GRID_Y, GRID_X), 1.0, 6.0, ((0, 32), (1, 8)), (0, 2, 32, 2.75))
    maps = centred(streams_of[1], (COMPONENTS, GRID_Z, GRID_Y, GRID_X), 1.0, 4.0, ((0, 2), (1, 8)))
    gram_old = draw_gram_old(jax.random.fold_in(streams_of[5], 71), 0)
    stats_old = centred(streams_of[3], (COMPONENTS, GRID_Z, GRID_Y, GRID_X), 1.0, 6.0, ((0, 2), (1, 8), (2, 32)), jnp.float32)
    kept = draw_kept(jax.random.fold_in(streams_of[5], 71), 0)
    return dict(scans=scans, maps=maps, gram_old=gram_old, stats_old=stats_old, kept=kept)


def smooth(field):
    padded = jnp.pad(field, ((0, 0), (1, 1), (1, 1), (1, 1)))
    lap_z = padded[:, 2:, 1:-1, 1:-1] + padded[:, :-2, 1:-1, 1:-1] - 2.0 * field
    lap_y = padded[:, 1:-1, 2:, 1:-1] + padded[:, 1:-1, :-2, 1:-1] - 2.0 * field
    lap_x = padded[:, 1:-1, 1:-1, 2:] + padded[:, 1:-1, 1:-1, :-2] - 2.0 * field
    return field + 0.24 * lap_z + 0.18 * lap_y + 0.12 * lap_x

def reference(scans, maps, gram_old, stats_old, kept):
    highest = lax.Precision.HIGHEST
    flat_scans = scans.reshape(ROWS, VOXELS)
    flat_maps = maps.reshape(COMPONENTS, VOXELS)
    proj = jnp.dot(flat_scans, flat_maps.T, preferred_element_type=jnp.float32) * (1.0 / math.sqrt(VOXELS))
    gram = jnp.dot(flat_maps, flat_maps.T, preferred_element_type=jnp.float32) * (1.0 / VOXELS)
    codes = 0.1 * proj
    for step in range(ITERS - 1):
        codes = codes + 0.1 * (proj - jnp.dot(codes, gram, precision=highest) - 0.2 * codes)
    rows = jnp.arange(ROWS, dtype=jnp.int32)
    subject = rows // VOLUMES
    within = rows % VOLUMES
    live = (within < kept[subject]).astype(jnp.float32)
    weighted = codes * live[:, None]
    gram_new = 0.5 * gram_old + 0.5 / ROWS * jnp.dot(weighted.T, codes, precision=highest)
    weighted_low = weighted.astype(jnp.bfloat16)
    term = jnp.dot(weighted_low.T, flat_scans, preferred_element_type=jnp.float32)
    stats_new = 0.5 * stats_old + 0.5 / math.sqrt(ROWS) * term.reshape(COMPONENTS, GRID_Z, GRID_Y, GRID_X)
    maps_wide = maps.astype(jnp.float32)
    coupled = jnp.dot(gram_new, maps_wide.reshape(COMPONENTS, VOXELS), precision=highest)
    diag = jnp.diagonal(gram_new)
    updated = maps_wide + (stats_new - coupled.reshape(COMPONENTS, GRID_Z, GRID_Y, GRID_X)) / diag[:, None, None, None]
    maps_new = smooth(updated).astype(jnp.bfloat16)
    return (maps_new, stats_new, gram_new, codes)
```

```python
import math

import jax
import jax.numpy as jnp
from jax import lax
from jax.sharding import PartitionSpec as P

COMPONENTS = 256
ITERS = 12
X_SIZE = 4
Y_SIZE = 8
LOW = jnp.bfloat16
WIDE = jnp.float32


def power_sum(gram):
    dot = lambda a, b: jnp.dot(a, b, precision=lax.Precision.HIGHEST)
    eye = jnp.eye(COMPONENTS, dtype=WIDE)
    first = 0.98 * eye - 0.1 * gram
    second = dot(first, first)
    third = dot(second, first)
    sum3 = eye + first + second
    sum6 = sum3 + dot(third, sum3)
    sixth = dot(third, third)
    return 0.1 * (sum6 + dot(sixth, sum6))


def on_device(scans, maps, gram_old, stats_old, kept):
    highest = lax.Precision.HIGHEST
    slabs = lax.axis_size("slab")
    subjects = lax.axis_size("subj")
    volumes = scans.shape[0]
    own_count, _, lines, width = maps.shape
    voxel_total = slabs * lines * width
    total_rows = volumes * subjects
    slab, subj, comp = lax.axis_index("slab"), lax.axis_index("subj"), lax.axis_index("comp")
    at_x = subj // Y_SIZE
    ring = slabs * X_SIZE * 2
    ring_groups = [
        [(s * subjects + x * Y_SIZE + y) * 2 + c for s in range(slabs) for x in range(X_SIZE) for c in range(2)]
        for y in range(Y_SIZE)
    ]
    x_groups = [[x * Y_SIZE + y for x in range(X_SIZE)] for y in range(Y_SIZE)]
    y_groups = [[x * Y_SIZE + y for y in range(Y_SIZE)] for x in range(X_SIZE)]
    whole_axes = ("slab", "subj", "comp")

    scans3 = scans.reshape(volumes, lines, width)
    maps3 = maps.reshape(own_count, lines, width)
    half = Y_SIZE // 2
    own_line = lax.dynamic_slice_in_dim(maps3, subj, 1, 1)
    to_partner = lax.dynamic_slice_in_dim(maps3, at_x * Y_SIZE + (1 - comp) * half, half, 1)
    got = lax.ppermute(jnp.concatenate([to_partner, own_line], axis=1), "comp", [(0, 1), (1, 0)])

    proj_part = jnp.einsum("ryx,kyx->rk", scans3, maps3, preferred_element_type=WIDE)
    proj_part = (proj_part * (1.0 / math.sqrt(voxel_total))).astype(LOW)

    quarter = lax.dynamic_slice_in_dim(maps3, at_x * Y_SIZE, Y_SIZE, 1)
    own_half = lax.dynamic_slice_in_dim(maps3, at_x * Y_SIZE + comp * half, half, 1)
    gram_own = jnp.einsum("ayx,byx->ab", quarter, quarter, preferred_element_type=WIDE)
    first = jnp.where(comp == 0, own_half, got[:, :half])
    second = jnp.where(comp == 0, got[:, :half], own_half)
    gram_cross = jnp.einsum("ayx,byx->ab", first, second, preferred_element_type=WIDE)
    gram_parts = jnp.concatenate(
        [gram_own.reshape(ring, -1, own_count), gram_cross.reshape(ring, -1, own_count)], axis=1
    )
    gram_parts = (gram_parts * (1.0 / voxel_total)).astype(LOW)

    pieces = volumes // 8
    proj_sent = jnp.pad(proj_part.reshape(pieces, 8, own_count), ((0, ring - pieces), (0, 0), (0, 0)))
    sent = jnp.concatenate([proj_sent, jnp.pad(gram_parts, ((0, 0), (0, 4), (0, 0)))], axis=1)
    taken = lax.all_to_all(sent, whole_axes, 0, 0, axis_index_groups=ring_groups)
    taken = taken.reshape(slabs, X_SIZE, 2, 16, own_count).astype(WIDE)
    slab_sum = taken.sum(0)
    proj_rows = slab_sum[:, :, :8].reshape(X_SIZE, 16, own_count)
    gram_rows = slab_sum[:, :, 8:12].sum(0)
    shared = jnp.concatenate([gram_rows[:, :2].reshape(4, own_count), gram_rows[:, 2:].sum(0)], axis=0)
    shared = jnp.pad(shared, ((0, 2), (0, 0)))
    back = jnp.concatenate([proj_rows, jnp.broadcast_to(shared, (X_SIZE, 8, own_count))], axis=1).astype(LOW)
    back = jnp.broadcast_to(back[None, :, None], (slabs, X_SIZE, 2, 24, own_count)).reshape(ring, 24, own_count)
    back = lax.all_to_all(back, whole_axes, 0, 0, axis_index_groups=ring_groups)
    proj = jnp.concatenate(
        [back[:pieces, :8].reshape(volumes, own_count), back[:pieces, 8:16].reshape(volumes, own_count)], axis=1
    )
    low_block = back[:, 16:18].reshape(own_count, own_count)
    high_block = back[:, 18:20].reshape(own_count, own_count)
    cross = back[:, 20:22].reshape(own_count, own_count)
    gram = jnp.concatenate(
        [jnp.concatenate([low_block, cross], axis=1), jnp.concatenate([cross.T, high_block], axis=1)], axis=0
    ).astype(WIDE)

    whole = jnp.dot(proj.astype(WIDE), power_sum(gram), precision=highest)
    codes = lax.dynamic_slice_in_dim(whole, comp * own_count, own_count, 1)
    live = (lax.iota(jnp.int32, volumes) < kept[0]).astype(WIDE)
    weighted_low = (codes * live[:, None]).astype(LOW)

    term = jnp.einsum("rk,ryx->ykx", weighted_low, scans3, preferred_element_type=WIDE)
    term = (term * (0.5 / math.sqrt(total_rows))).astype(LOW).reshape(X_SIZE, Y_SIZE * own_count, width)
    product = jnp.dot(weighted_low.T, whole.astype(LOW), preferred_element_type=WIDE) * (0.5 / total_rows)
    share = own_count // slabs
    mine = lax.dynamic_slice_in_dim(product, slab * share, share, 0).astype(LOW)
    mine = jnp.concatenate([mine[:, :own_count], mine[:, own_count:]], axis=0)
    sent = jnp.concatenate([term, jnp.broadcast_to(mine, (X_SIZE, 2 * share, width))], axis=1)
    taken = lax.all_to_all(sent, "subj", 0, 0, axis_index_groups=x_groups).astype(WIDE).sum(0).astype(LOW)
    sent = jnp.concatenate(
        [
            taken[: Y_SIZE * own_count].reshape(Y_SIZE, own_count, width),
            jnp.broadcast_to(taken[Y_SIZE * own_count :], (Y_SIZE, 2 * share, width)),
        ],
        axis=1,
    )
    summed = lax.all_to_all(sent, "subj", 0, 0, axis_index_groups=y_groups).astype(WIDE).sum(0)
    stats_line = 0.5 * stats_old.reshape(own_count, width) + summed[:own_count]
    mine = jnp.broadcast_to(summed[own_count:].astype(LOW), (slabs, 2 * share, width))
    product = lax.all_to_all(mine, "slab", 0, 0).astype(WIDE)
    product = jnp.concatenate(
        [product[:, :share].reshape(own_count, own_count), product[:, share:].reshape(own_count, own_count)], axis=1
    )
    gram_new = 0.5 * gram_old + product

    own_piece = own_line.reshape(own_count, width)
    other_piece = got[:, half]
    piece = jnp.where(
        comp == 0,
        jnp.concatenate([own_piece, other_piece], axis=0),
        jnp.concatenate([other_piece, own_piece], axis=0),
    ).astype(WIDE)
    block = lax.dynamic_slice_in_dim(gram_new, comp * own_count, own_count, 1)
    diag = jnp.sum(block * jnp.eye(own_count, dtype=WIDE), axis=1, keepdims=True)
    coupled = jnp.dot(gram_new, piece, precision=highest)
    updated = own_piece.astype(WIDE) + (stats_line - coupled) / diag
    edge = updated.astype(LOW)
    sides = []
    for axis in ("slab", "subj"):
        count = lax.axis_size(axis)
        up = [(i, i + 1) for i in range(count - 1)]
        sides.append(lax.ppermute(edge, axis, up) + 0.0)
        sides.append(lax.ppermute(edge, axis, [(b, a) for a, b in up]) + 0.0)
    z_low, z_high, y_low, y_high = [side.astype(WIDE) for side in sides]
    side_x = jnp.pad(updated, ((0, 0), (1, 1)))
    lap_x = side_x[:, 2:] + side_x[:, :-2] - 2.0 * updated
    lap_z = z_low + z_high - 2.0 * updated
    lap_y = y_low + y_high - 2.0 * updated
    maps_new = (updated + 0.24 * lap_z + 0.18 * lap_y + 0.12 * lap_x).astype(LOW)
    return (
        maps_new.reshape(own_count, 1, 1, width),
        stats_line.reshape(own_count, 1, 1, width),
        gram_new,
        codes,
    )


def solution(mesh):
    in_specs = (
        P("subj", "slab", None, None),
        P("comp", "slab", None, None),
        P("comp", None),
        P("comp", "slab", "subj", None),
        P("subj"),
    )
    out_specs = (
        P("comp", "slab", "subj", None),
        P("comp", "slab", "subj", None),
        P("comp", None),
        P("subj", "comp"),
    )
    return jax.shard_map(
        on_device, mesh=mesh, in_specs=in_specs, out_specs=out_specs, check_vma=False
    )
```

```python
import math

import jax
import jax.numpy as jnp
from jax import lax
from jax.sharding import PartitionSpec as P

COMPONENTS = 256
ITERS = 12
X_SIZE = 4
Y_SIZE = 8
LOW = jnp.bfloat16
WIDE = jnp.float32


def power_sum(gram):
    dot = lambda a, b: jnp.dot(a, b, precision=lax.Precision.HIGHEST)
    eye = jnp.eye(COMPONENTS, dtype=WIDE)
    first = 0.98 * eye - 0.1 * gram
    second = dot(first, first)
    third = dot(second, first)
    sum3 = eye + first + second
    sum6 = sum3 + dot(third, sum3)
    sixth = dot(third, third)
    return 0.1 * (sum6 + dot(sixth, sum6))


def on_device(scans, maps, gram_old, stats_old, kept):
    highest = lax.Precision.HIGHEST
    slabs = lax.axis_size("slab")
    subjects = lax.axis_size("subj")
    volumes = scans.shape[0]
    own_count, _, lines, width = maps.shape
    voxel_total = slabs * lines * width
    total_rows = volumes * subjects
    slab, subj, comp = lax.axis_index("slab"), lax.axis_index("subj"), lax.axis_index("comp")
    at_x = subj // Y_SIZE
    ring = slabs * X_SIZE * 2
    ring_groups = [
        [(s * subjects + x * Y_SIZE + y) * 2 + c for s in range(slabs) for x in range(X_SIZE) for c in range(2)]
        for y in range(Y_SIZE)
    ]
    x_groups = [[x * Y_SIZE + y for x in range(X_SIZE)] for y in range(Y_SIZE)]
    y_groups = [[x * Y_SIZE + y for y in range(Y_SIZE)] for x in range(X_SIZE)]
    whole_axes = ("slab", "subj", "comp")

    scans3 = scans.reshape(volumes, lines, width)
    maps3 = maps.reshape(own_count, lines, width)
    half = Y_SIZE // 2
    own_line = lax.dynamic_slice_in_dim(maps3, subj, 1, 1)
    to_partner = lax.dynamic_slice_in_dim(maps3, at_x * Y_SIZE + (1 - comp) * half, half, 1)
    got = lax.ppermute(jnp.concatenate([to_partner, own_line], axis=1), "comp", [(0, 1), (1, 0)])

    proj_part = jnp.einsum("ryx,kyx->rk", scans3, maps3, preferred_element_type=WIDE)
    proj_part = (proj_part * (1.0 / math.sqrt(voxel_total))).astype(LOW)

    quarter = lax.dynamic_slice_in_dim(maps3, at_x * Y_SIZE, Y_SIZE, 1)
    own_half = lax.dynamic_slice_in_dim(maps3, at_x * Y_SIZE + comp * half, half, 1)
    gram_own = jnp.einsum("ayx,byx->ab", quarter, quarter, preferred_element_type=WIDE)
    first = jnp.where(comp == 0, own_half, got[:, :half])
    second = jnp.where(comp == 0, got[:, :half], own_half)
    gram_cross = jnp.einsum("ayx,byx->ab", first, second, preferred_element_type=WIDE)
    gram_parts = jnp.concatenate(
        [gram_own.reshape(ring, -1, own_count), gram_cross.reshape(ring, -1, own_count)], axis=1
    )
    gram_parts = (gram_parts * (1.0 / voxel_total)).astype(LOW)

    pieces = volumes // 8
    proj_sent = jnp.pad(proj_part.reshape(pieces, 8, own_count), ((0, ring - pieces), (0, 0), (0, 0)))
    sent = jnp.concatenate([proj_sent, jnp.pad(gram_parts, ((0, 0), (0, 4), (0, 0)))], axis=1)
    taken = lax.all_to_all(sent, whole_axes, 0, 0, axis_index_groups=ring_groups)
    taken = taken.reshape(slabs, X_SIZE, 2, 16, own_count).astype(WIDE)
    slab_sum = taken.sum(0)
    proj_rows = slab_sum[:, :, :8].reshape(X_SIZE, 16, own_count)
    gram_rows = slab_sum[:, :, 8:12].sum(0)
    shared = jnp.concatenate([gram_rows[:, :2].reshape(4, own_count), gram_rows[:, 2:].sum(0)], axis=0)
    shared = jnp.pad(shared, ((0, 2), (0, 0)))
    back = jnp.concatenate([proj_rows, jnp.broadcast_to(shared, (X_SIZE, 8, own_count))], axis=1).astype(LOW)
    back = jnp.broadcast_to(back[None, :, None], (slabs, X_SIZE, 2, 24, own_count)).reshape(ring, 24, own_count)
    back = lax.all_to_all(back, whole_axes, 0, 0, axis_index_groups=ring_groups)
    back, kept, scans3 = lax.optimization_barrier((back, kept, scans3))
    proj = jnp.concatenate(
        [back[:pieces, :8].reshape(volumes, own_count), back[:pieces, 8:16].reshape(volumes, own_count)], axis=1
    )
    low_block = back[:, 16:18].reshape(own_count, own_count)
    high_block = back[:, 18:20].reshape(own_count, own_count)
    cross = back[:, 20:22].reshape(own_count, own_count)
    gram = jnp.concatenate(
        [jnp.concatenate([low_block, cross], axis=1), jnp.concatenate([cross.T, high_block], axis=1)], axis=0
    ).astype(WIDE)

    whole = jnp.dot(proj.astype(WIDE), power_sum(gram), precision=highest)
    codes = lax.dynamic_slice_in_dim(whole, comp * own_count, own_count, 1)
    live = (lax.iota(jnp.int32, volumes) < kept[0]).astype(WIDE)
    weighted_low = (codes * live[:, None]).astype(LOW)

    term = jnp.einsum("rk,ryx->ykx", weighted_low, scans3, preferred_element_type=WIDE)
    term = (term * (0.5 / math.sqrt(total_rows))).astype(LOW).reshape(X_SIZE, Y_SIZE * own_count, width)
    product = jnp.dot(weighted_low.T, whole.astype(LOW), preferred_element_type=WIDE) * (0.5 / total_rows)
    share = own_count // slabs
    mine = lax.dynamic_slice_in_dim(product, slab * share, share, 0).astype(LOW)
    mine = jnp.concatenate([mine[:, :own_count], mine[:, own_count:]], axis=0)
    sent = jnp.concatenate([term, jnp.broadcast_to(mine, (X_SIZE, 2 * share, width))], axis=1)
    taken = lax.all_to_all(sent, "subj", 0, 0, axis_index_groups=x_groups).astype(WIDE).sum(0).astype(LOW)
    sent = jnp.concatenate(
        [
            taken[: Y_SIZE * own_count].reshape(Y_SIZE, own_count, width),
            jnp.broadcast_to(taken[Y_SIZE * own_count :], (Y_SIZE, 2 * share, width)),
        ],
        axis=1,
    )
    summed = lax.all_to_all(sent, "subj", 0, 0, axis_index_groups=y_groups)
    summed, stats_old, gram_old = lax.optimization_barrier((summed, stats_old, gram_old))
    summed = summed.astype(WIDE).sum(0)
    mine = jnp.broadcast_to(summed[own_count:].astype(LOW), (slabs, 2 * share, width))
    product = lax.all_to_all(mine, "slab", 0, 0)
    product, summed, stats_old, got, own_line = lax.optimization_barrier((product, summed, stats_old, got, own_line))
    product = product.astype(WIDE)
    product = jnp.concatenate(
        [product[:, :share].reshape(own_count, own_count), product[:, share:].reshape(own_count, own_count)], axis=1
    )
    gram_new = 0.5 * gram_old + product
    stats_line = 0.5 * stats_old.reshape(own_count, width) + summed[:own_count]

    own_piece = own_line.reshape(own_count, width)
    other_piece = got[:, half]
    piece = jnp.where(
        comp == 0,
        jnp.concatenate([own_piece, other_piece], axis=0),
        jnp.concatenate([other_piece, own_piece], axis=0),
    ).astype(WIDE)
    block = lax.dynamic_slice_in_dim(gram_new, comp * own_count, own_count, 1)
    diag = jnp.sum(block * jnp.eye(own_count, dtype=WIDE), axis=1, keepdims=True)
    coupled = jnp.dot(gram_new, piece, precision=highest)
    updated = own_piece.astype(WIDE) + (stats_line - coupled) / diag
    edge = updated.astype(LOW)
    sides = []
    for axis in ("slab", "subj"):
        count = lax.axis_size(axis)
        up = [(i, i + 1) for i in range(count - 1)]
        sides.append(lax.ppermute(edge, axis, up) + 0.0)
        sides.append(lax.ppermute(edge, axis, [(b, a) for a, b in up]) + 0.0)
    z_low, z_high, y_low, y_high = [side.astype(WIDE) for side in sides]
    side_x = jnp.pad(updated, ((0, 0), (1, 1)))
    lap_x = side_x[:, 2:] + side_x[:, :-2] - 2.0 * updated
    lap_z = z_low + z_high - 2.0 * updated
    lap_y = y_low + y_high - 2.0 * updated
    maps_new = (updated + 0.24 * lap_z + 0.18 * lap_y + 0.12 * lap_x).astype(LOW)
    return (
        maps_new.reshape(own_count, 1, 1, width),
        stats_line.reshape(own_count, 1, 1, width),
        gram_new,
        codes,
    )


def solution(mesh):
    in_specs = (
        P("subj", "slab", None, None),
        P("comp", "slab", None, None),
        P("comp", None),
        P("comp", "slab", "subj", None),
        P("subj"),
    )
    out_specs = (
        P("comp", "slab", "subj", None),
        P("comp", "slab", "subj", None),
        P("comp", None),
        P("subj", "comp"),
    )
    return jax.shard_map(
        on_device, mesh=mesh, in_specs=in_specs, out_specs=out_specs, check_vma=False
    )
```

```python
import math

import jax
import jax.numpy as jnp
from jax import lax
from jax.sharding import PartitionSpec as P

COMPONENTS = 256
ITERS = 12
X_SIZE = 4
Y_SIZE = 8
LOW = jnp.bfloat16
WIDE = jnp.float32


def power_sum(gram):
    dot = lambda a, b: jnp.dot(a, b, precision=lax.Precision.HIGHEST)
    eye = jnp.eye(COMPONENTS, dtype=WIDE)
    first = 0.98 * eye - 0.1 * gram
    second = dot(first, first)
    third = dot(second, first)
    sum3 = eye + first + second
    sum6 = sum3 + dot(third, sum3)
    sixth = dot(third, third)
    return 0.1 * (sum6 + dot(sixth, sum6))


def on_device(scans, maps, gram_old, stats_old, kept):
    highest = lax.Precision.HIGHEST
    slabs = lax.axis_size("slab")
    subjects = lax.axis_size("subj")
    volumes = scans.shape[0]
    own_count, _, lines, width = maps.shape
    voxel_total = slabs * lines * width
    total_rows = volumes * subjects
    slab, subj, comp = lax.axis_index("slab"), lax.axis_index("subj"), lax.axis_index("comp")
    half_at = (subj // Y_SIZE) % 2
    ring = slabs * 4
    ring_groups = [
        [(s * subjects + (2 * pair + h) * Y_SIZE + y) * 2 + c for s in range(slabs) for h in range(2) for c in range(2)]
        for pair in range(X_SIZE // 2)
        for y in range(Y_SIZE)
    ]
    x_groups = [[x * Y_SIZE + y for x in range(X_SIZE)] for y in range(Y_SIZE)]
    y_groups = [[x * Y_SIZE + y for y in range(Y_SIZE)] for x in range(X_SIZE)]
    whole_axes = ("slab", "subj", "comp")

    scans3 = scans.reshape(volumes, lines, width)
    maps3 = maps.reshape(own_count, lines, width)
    part = lines // 4
    own_line = lax.dynamic_slice_in_dim(maps3, subj, 1, 1)
    to_partner = lax.dynamic_slice_in_dim(maps3, half_at * 2 * part + (1 - comp) * part, part, 1)
    got = lax.ppermute(jnp.concatenate([to_partner, own_line], axis=1), "comp", [(0, 1), (1, 0)])

    proj_part = jnp.einsum("ryx,kyx->rk", scans3, maps3, preferred_element_type=WIDE)
    proj_part = (proj_part * (1.0 / math.sqrt(voxel_total))).astype(LOW)

    own_lines = lax.dynamic_slice_in_dim(maps3, half_at * 2 * part, 2 * part, 1)
    own_half = lax.dynamic_slice_in_dim(maps3, half_at * 2 * part + comp * part, part, 1)
    gram_own = jnp.einsum("ayx,byx->ab", own_lines, own_lines, preferred_element_type=WIDE)
    first = jnp.where(comp == 0, own_half, got[:, :part])
    second = jnp.where(comp == 0, got[:, :part], own_half)
    gram_cross = jnp.einsum("ayx,byx->ab", first, second, preferred_element_type=WIDE)
    gram_parts = jnp.concatenate(
        [gram_own.reshape(ring, -1, own_count), gram_cross.reshape(ring, -1, own_count)], axis=1
    )
    gram_parts = (gram_parts * (1.0 / voxel_total)).astype(LOW)

    rows = 16
    pieces = volumes // rows
    few = own_count // ring
    proj_sent = jnp.pad(proj_part.reshape(pieces, rows, own_count), ((0, ring - pieces), (0, 0), (0, 0)))
    sent = jnp.concatenate([proj_sent, gram_parts], axis=1)
    taken = lax.all_to_all(sent, whole_axes, 0, 0, axis_index_groups=ring_groups)
    taken = taken.reshape(slabs, 2, 2, rows + 2 * few, own_count).astype(WIDE)
    slab_sum = taken.sum(0)
    proj_rows = slab_sum[:, :, :rows].reshape(2, 2 * rows, own_count)
    gram_rows = slab_sum[:, :, rows:].sum(0)
    shared = jnp.concatenate([gram_rows[:, :few].reshape(2 * few, own_count), gram_rows[:, few:].sum(0)], axis=0)
    shared = jnp.pad(shared, ((0, few), (0, 0)))
    back = jnp.concatenate([proj_rows, jnp.broadcast_to(shared, (2,) + shared.shape)], axis=1).astype(LOW)
    height = back.shape[1]
    back = jnp.broadcast_to(back[None, :, None], (slabs, 2, 2, height, own_count)).reshape(ring, height, own_count)
    back = lax.all_to_all(back, whole_axes, 0, 0, axis_index_groups=ring_groups)
    back, kept, scans3 = lax.optimization_barrier((back, kept, scans3))
    proj = jnp.concatenate(
        [back[:pieces, i * rows : (i + 1) * rows].reshape(volumes, own_count) for i in range(2)], axis=1
    )
    low_block, high_block, cross = [
        back[:, 2 * rows + i * few : 2 * rows + (i + 1) * few].reshape(own_count, own_count) for i in range(3)
    ]
    gram = jnp.concatenate(
        [jnp.concatenate([low_block, cross], axis=1), jnp.concatenate([cross.T, high_block], axis=1)], axis=0
    ).astype(WIDE)

    whole = jnp.dot(proj.astype(WIDE), power_sum(gram), precision=highest)
    codes = lax.dynamic_slice_in_dim(whole, comp * own_count, own_count, 1)
    live = (lax.iota(jnp.int32, volumes) < kept[0]).astype(WIDE)
    weighted_low = (codes * live[:, None]).astype(LOW)

    term = jnp.einsum("rk,ryx->ykx", weighted_low, scans3, preferred_element_type=WIDE)
    term = (term * (0.5 / math.sqrt(total_rows))).astype(LOW).reshape(X_SIZE, Y_SIZE * own_count, width)
    product = jnp.dot(weighted_low.T, whole.astype(LOW), preferred_element_type=WIDE) * (0.5 / total_rows)
    product = jnp.concatenate([product[:, :own_count], product[:, own_count:]], axis=0).astype(LOW)
    sent = jnp.concatenate([term, jnp.broadcast_to(product, (X_SIZE,) + product.shape)], axis=1)
    taken = lax.all_to_all(sent, "subj", 0, 0, axis_index_groups=x_groups).astype(WIDE).sum(0).astype(LOW)
    split = Y_SIZE * own_count
    sent = jnp.concatenate(
        [
            taken[:split].reshape(Y_SIZE, own_count, width),
            jnp.broadcast_to(taken[split:], (Y_SIZE, 2 * own_count, width)),
        ],
        axis=1,
    )
    summed = lax.all_to_all(sent, "subj", 0, 0, axis_index_groups=y_groups)
    summed, stats_old, gram_old, got, own_line = lax.optimization_barrier((summed, stats_old, gram_old, got, own_line))
    summed = summed.astype(WIDE).sum(0)
    product = jnp.concatenate([summed[own_count : 2 * own_count], summed[2 * own_count :]], axis=1)
    gram_new = 0.5 * gram_old + product
    stats_line = 0.5 * stats_old.reshape(own_count, width) + summed[:own_count]

    own_piece = own_line.reshape(own_count, width)
    other_piece = got[:, part]
    piece = jnp.where(
        comp == 0,
        jnp.concatenate([own_piece, other_piece], axis=0),
        jnp.concatenate([other_piece, own_piece], axis=0),
    ).astype(WIDE)
    block = lax.dynamic_slice_in_dim(gram_new, comp * own_count, own_count, 1)
    diag = jnp.sum(block * jnp.eye(own_count, dtype=WIDE), axis=1, keepdims=True)
    coupled = jnp.dot(gram_new, piece, precision=highest)
    updated = own_piece.astype(WIDE) + (stats_line - coupled) / diag
    edge = updated.astype(LOW)
    sides = []
    for axis in ("slab", "subj"):
        count = lax.axis_size(axis)
        up = [(i, i + 1) for i in range(count - 1)]
        sides.append(lax.ppermute(edge, axis, up) + 0.0)
        sides.append(lax.ppermute(edge, axis, [(b, a) for a, b in up]) + 0.0)
    z_low, z_high, y_low, y_high = [side.astype(WIDE) for side in sides]
    side_x = jnp.pad(updated, ((0, 0), (1, 1)))
    lap_x = side_x[:, 2:] + side_x[:, :-2] - 2.0 * updated
    lap_z = z_low + z_high - 2.0 * updated
    lap_y = y_low + y_high - 2.0 * updated
    maps_new = (updated + 0.24 * lap_z + 0.18 * lap_y + 0.12 * lap_x).astype(LOW)
    return (
        maps_new.reshape(own_count, 1, 1, width),
        stats_line.reshape(own_count, 1, 1, width),
        gram_new,
        codes,
    )


def solution(mesh):
    in_specs = (
        P("subj", "slab", None, None),
        P("comp", "slab", None, None),
        P("comp", None),
        P("comp", "slab", "subj", None),
        P("subj"),
    )
    out_specs = (
        P("comp", "slab", "subj", None),
        P("comp", "slab", "subj", None),
        P("comp", None),
        P("subj", "comp"),
    )
    return jax.shard_map(
        on_device, mesh=mesh, in_specs=in_specs, out_specs=out_specs, check_vma=False
    )
```

```python
import math

import jax
import jax.numpy as jnp
from jax import lax
from jax.sharding import PartitionSpec as P

COMPONENTS = 256
ITERS = 12
X_SIZE = 4
Y_SIZE = 8
LOW = jnp.bfloat16
WIDE = jnp.float32


def power_sum(gram):
    dot = lambda a, b: jnp.dot(a, b, precision=lax.Precision.HIGHEST)
    eye = jnp.eye(COMPONENTS, dtype=WIDE)
    first = 0.98 * eye - 0.1 * gram
    second = dot(first, first)
    third = dot(second, first)
    sum3 = eye + first + second
    sum6 = sum3 + dot(third, sum3)
    sixth = dot(third, third)
    return 0.1 * (sum6 + dot(sixth, sum6))


def on_device(scans, maps, gram_old, stats_old, kept):
    highest = lax.Precision.HIGHEST
    slabs = lax.axis_size("slab")
    subjects = lax.axis_size("subj")
    volumes = scans.shape[0]
    own_count, _, lines, width = maps.shape
    voxel_total = slabs * lines * width
    total_rows = volumes * subjects
    slab, subj, comp = lax.axis_index("slab"), lax.axis_index("subj"), lax.axis_index("comp")
    half_at = (subj // Y_SIZE) % 2
    ring = slabs * 4
    ring_groups = [
        [(s * subjects + (2 * pair + h) * Y_SIZE + y) * 2 + c for s in range(slabs) for h in range(2) for c in range(2)]
        for pair in range(X_SIZE // 2)
        for y in range(Y_SIZE)
    ]
    x_groups = [[x * Y_SIZE + y for x in range(X_SIZE)] for y in range(Y_SIZE)]
    y_groups = [[x * Y_SIZE + y for y in range(Y_SIZE)] for x in range(X_SIZE)]
    whole_axes = ("slab", "subj", "comp")

    scans3 = scans.reshape(volumes, lines, width)
    maps3 = maps.reshape(own_count, lines, width)
    part = lines // 4
    own_line = lax.dynamic_slice_in_dim(maps3, subj, 1, 1)
    to_partner = lax.dynamic_slice_in_dim(maps3, half_at * 2 * part + (1 - comp) * part, part, 1)
    got = lax.ppermute(jnp.concatenate([to_partner, own_line], axis=1), "comp", [(0, 1), (1, 0)])

    proj_part = jnp.einsum("ryx,kyx->rk", scans3, maps3, preferred_element_type=WIDE)
    proj_part = (proj_part * (1.0 / math.sqrt(voxel_total))).astype(LOW)

    own_lines = lax.dynamic_slice_in_dim(maps3, half_at * 2 * part, 2 * part, 1)
    own_half = lax.dynamic_slice_in_dim(maps3, half_at * 2 * part + comp * part, part, 1)
    gram_own = jnp.einsum("ayx,byx->ab", own_lines, own_lines, preferred_element_type=WIDE)
    first = jnp.where(comp == 0, own_half, got[:, :part])
    second = jnp.where(comp == 0, got[:, :part], own_half)
    gram_cross = jnp.einsum("ayx,byx->ab", first, second, preferred_element_type=WIDE)
    gram_parts = jnp.concatenate(
        [gram_own.reshape(ring, -1, own_count), gram_cross.reshape(ring, -1, own_count)], axis=1
    )
    gram_parts = (gram_parts * (1.0 / voxel_total)).astype(LOW)

    rows = 16
    pieces = volumes // rows
    few = own_count // ring
    proj_sent = jnp.pad(proj_part.reshape(pieces, rows, own_count), ((0, ring - pieces), (0, 0), (0, 0)))
    sent = jnp.concatenate([proj_sent, gram_parts], axis=1)
    taken = lax.all_to_all(sent, whole_axes, 0, 0, axis_index_groups=ring_groups)
    taken = taken.reshape(slabs, 2, 2, rows + 2 * few, own_count).astype(WIDE)
    slab_sum = taken.sum(0)
    proj_rows = slab_sum[:, :, :rows].reshape(2, 2 * rows, own_count)
    gram_rows = slab_sum[:, :, rows:].sum(0)
    shared = jnp.concatenate([gram_rows[:, :few].reshape(2 * few, own_count), gram_rows[:, few:].sum(0)], axis=0)
    shared = jnp.pad(shared, ((0, few), (0, 0)))
    back = jnp.concatenate([proj_rows, jnp.broadcast_to(shared, (2,) + shared.shape)], axis=1).astype(LOW)
    height = back.shape[1]
    back = jnp.broadcast_to(back[None, :, None], (slabs, 2, 2, height, own_count)).reshape(ring, height, own_count)
    back = lax.all_to_all(back, whole_axes, 0, 0, axis_index_groups=ring_groups)
    back, kept, scans3 = lax.optimization_barrier((back, kept, scans3))
    proj = jnp.concatenate(
        [back[:pieces, i * rows : (i + 1) * rows].reshape(volumes, own_count) for i in range(2)], axis=1
    )
    low_block, high_block, cross = [
        back[:, 2 * rows + i * few : 2 * rows + (i + 1) * few].reshape(own_count, own_count) for i in range(3)
    ]
    gram = jnp.concatenate(
        [jnp.concatenate([low_block, cross], axis=1), jnp.concatenate([cross.T, high_block], axis=1)], axis=0
    ).astype(WIDE)

    whole = jnp.dot(proj.astype(WIDE), power_sum(gram), precision=highest)
    codes = lax.dynamic_slice_in_dim(whole, comp * own_count, own_count, 1)
    live = (lax.iota(jnp.int32, volumes) < kept[0]).astype(WIDE)
    weighted_low = (codes * live[:, None]).astype(LOW)

    term = jnp.einsum("rk,ryx->ykx", weighted_low, scans3, preferred_element_type=WIDE)
    term = (term * (0.5 / math.sqrt(total_rows))).astype(LOW).reshape(X_SIZE, Y_SIZE * own_count, width)
    product = jnp.dot(weighted_low.T, whole.astype(LOW), preferred_element_type=WIDE) * (0.5 / total_rows)
    share = own_count // slabs
    mine = lax.dynamic_slice_in_dim(product, slab * share, share, 0).astype(LOW)
    mine = jnp.concatenate([mine[:, :own_count], mine[:, own_count:]], axis=0)
    sent = jnp.concatenate([term, jnp.broadcast_to(mine, (X_SIZE, 2 * share, width))], axis=1)
    taken = lax.all_to_all(sent, "subj", 0, 0, axis_index_groups=x_groups).astype(WIDE).sum(0).astype(LOW)
    split = Y_SIZE * own_count
    sent = jnp.concatenate(
        [
            taken[:split].reshape(Y_SIZE, own_count, width),
            jnp.broadcast_to(taken[split:], (Y_SIZE, 2 * share, width)),
        ],
        axis=1,
    )
    summed = lax.all_to_all(sent, "subj", 0, 0, axis_index_groups=y_groups)
    summed, stats_old, gram_old = lax.optimization_barrier((summed, stats_old, gram_old))
    summed = summed.astype(WIDE).sum(0)
    mine = jnp.broadcast_to(summed[own_count:].astype(LOW), (slabs, 2 * share, width))
    product = lax.all_to_all(mine, "slab", 0, 0)
    product, summed, stats_old, got, own_line = lax.optimization_barrier((product, summed, stats_old, got, own_line))
    product = product.astype(WIDE)
    product = jnp.concatenate(
        [product[:, :share].reshape(own_count, own_count), product[:, share:].reshape(own_count, own_count)], axis=1
    )
    gram_new = 0.5 * gram_old + product
    stats_line = 0.5 * stats_old.reshape(own_count, width) + summed[:own_count]

    own_piece = own_line.reshape(own_count, width)
    other_piece = got[:, part]
    piece = jnp.where(
        comp == 0,
        jnp.concatenate([own_piece, other_piece], axis=0),
        jnp.concatenate([other_piece, own_piece], axis=0),
    ).astype(WIDE)
    block = lax.dynamic_slice_in_dim(gram_new, comp * own_count, own_count, 1)
    diag = jnp.sum(block * jnp.eye(own_count, dtype=WIDE), axis=1, keepdims=True)
    coupled = jnp.dot(gram_new, piece, precision=highest)
    updated = own_piece.astype(WIDE) + (stats_line - coupled) / diag
    edge = updated.astype(LOW)
    sides = []
    for axis in ("slab", "subj"):
        count = lax.axis_size(axis)
        up = [(i, i + 1) for i in range(count - 1)]
        sides.append(lax.ppermute(edge, axis, up) + 0.0)
        sides.append(lax.ppermute(edge, axis, [(b, a) for a, b in up]) + 0.0)
    z_low, z_high, y_low, y_high = [side.astype(WIDE) for side in sides]
    side_x = jnp.pad(updated, ((0, 0), (1, 1)))
    lap_x = side_x[:, 2:] + side_x[:, :-2] - 2.0 * updated
    lap_z = z_low + z_high - 2.0 * updated
    lap_y = y_low + y_high - 2.0 * updated
    maps_new = (updated + 0.24 * lap_z + 0.18 * lap_y + 0.12 * lap_x).astype(LOW)
    return (
        maps_new.reshape(own_count, 1, 1, width),
        stats_line.reshape(own_count, 1, 1, width),
        gram_new,
        codes,
    )


def solution(mesh):
    in_specs = (
        P("subj", "slab", None, None),
        P("comp", "slab", None, None),
        P("comp", None),
        P("comp", "slab", "subj", None),
        P("subj"),
    )
    out_specs = (
        P("comp", "slab", "subj", None),
        P("comp", "slab", "subj", None),
        P("comp", None),
        P("subj", "comp"),
    )
    return jax.shard_map(
        on_device, mesh=mesh, in_specs=in_specs, out_specs=out_specs, check_vma=False
    )
```

```python
import math

import jax
import jax.numpy as jnp
from jax import lax
from jax.sharding import PartitionSpec as P

COMPONENTS = 256
ITERS = 12
X_SIZE = 4
Y_SIZE = 8
LOW = jnp.bfloat16
WIDE = jnp.float32
SWAP = [(0, 1), (1, 0)]


def power_sum(gram):
    dot = lambda a, b: jnp.dot(a, b, precision=lax.Precision.HIGHEST)
    eye = jnp.eye(COMPONENTS, dtype=WIDE)
    first = 0.98 * eye - 0.1 * gram
    second = dot(first, first)
    third = dot(second, first)
    sum3 = eye + first + second
    sum6 = sum3 + dot(third, sum3)
    sixth = dot(third, third)
    return 0.1 * (sum6 + dot(sixth, sum6))


def on_device(scans, maps, gram_old, stats_old, kept):
    highest = lax.Precision.HIGHEST
    slabs = lax.axis_size("slab")
    subjects = lax.axis_size("subj")
    volumes = scans.shape[0]
    own_count, _, lines, width = maps.shape
    voxel_total = slabs * lines * width
    total_rows = volumes * subjects
    slab, subj, comp = lax.axis_index("slab"), lax.axis_index("subj"), lax.axis_index("comp")
    at_x = subj // Y_SIZE
    ring = slabs * 2
    ring_axes = ("slab", "comp")
    x_groups = [[x * Y_SIZE + y for x in range(X_SIZE)] for y in range(Y_SIZE)]
    y_groups = [[x * Y_SIZE + y for y in range(Y_SIZE)] for x in range(X_SIZE)]

    scans3 = scans.reshape(volumes, lines, width)
    maps3 = maps.reshape(own_count, lines, width)
    part = lines // (2 * X_SIZE)
    own_line = lax.dynamic_slice_in_dim(maps3, subj, 1, 1)
    to_partner = lax.dynamic_slice_in_dim(maps3, (2 * at_x + 1 - comp) * part, part, 1)
    got = lax.ppermute(jnp.concatenate([to_partner, own_line], axis=1), "comp", SWAP)

    proj_part = jnp.einsum("ryx,kyx->rk", scans3, maps3, preferred_element_type=WIDE)
    proj_part = (proj_part * (1.0 / math.sqrt(voxel_total))).astype(LOW)
    rows = 32
    pieces = volumes // rows
    few = own_count // ring
    sent = jnp.pad(proj_part.reshape(pieces, rows, own_count), ((0, ring - pieces), (0, 0), (0, 0)))
    taken = lax.all_to_all(sent, ring_axes, 0, 0)
    proj_rows = taken.reshape(slabs, 2, rows, own_count).astype(WIDE).sum(0).astype(LOW)

    own_lines = lax.dynamic_slice_in_dim(maps3, at_x * 2 * part, 2 * part, 1)
    own_half = lax.dynamic_slice_in_dim(maps3, (2 * at_x + comp) * part, part, 1)
    gram_own = jnp.einsum("ayx,byx->ab", own_lines, own_lines, preferred_element_type=WIDE)
    first = jnp.where(comp == 0, own_half, got[:, :part])
    second = jnp.where(comp == 0, got[:, :part], own_half)
    gram_cross = jnp.einsum("ayx,byx->ab", first, second, preferred_element_type=WIDE)
    gram_parts = jnp.concatenate(
        [gram_own.reshape(ring, few, own_count), gram_cross.reshape(ring, few, own_count)], axis=1
    )
    gram_parts = (gram_parts * (1.0 / voxel_total)).astype(LOW)
    proj_rows = jnp.broadcast_to(proj_rows.reshape(2 * rows, own_count), (ring, 2 * rows, own_count))
    back = lax.all_to_all(jnp.concatenate([proj_rows, gram_parts], axis=1), ring_axes, 0, 0)
    proj_pair = [back[:pieces, i * rows : (i + 1) * rows].reshape(volumes, own_count) for i in range(2)]
    proj = jnp.concatenate(proj_pair, axis=1)
    gram_rows = back[:, 2 * rows :].astype(WIDE).reshape(slabs, 2, 2 * few, own_count).sum(0)
    gram_rows = jnp.concatenate(
        [gram_rows[:, :few].reshape(2 * few, own_count), gram_rows[:, few:].sum(0)], axis=0
    ).astype(LOW)

    live = (lax.iota(jnp.int32, volumes) < kept[0]).astype(LOW)
    live_proj = jnp.where(comp == 0, proj_pair[0], proj_pair[1]) * live[:, None]
    term = jnp.einsum("rk,ryx->ykx", live_proj, scans3, preferred_element_type=WIDE)
    term = (term * (0.5 / math.sqrt(total_rows))).astype(LOW).reshape(X_SIZE, Y_SIZE * own_count, width)
    product = jnp.dot(live_proj.T, proj, preferred_element_type=WIDE) * (0.5 / total_rows)
    share = own_count // slabs
    mine = lax.dynamic_slice_in_dim(product, slab * share, share, 0).astype(LOW)
    mine = jnp.concatenate([mine[:, :own_count], mine[:, own_count:], gram_rows], axis=0)
    sent = jnp.concatenate([term, jnp.broadcast_to(mine, (X_SIZE,) + mine.shape)], axis=1)
    taken = lax.all_to_all(sent, "subj", 0, 0, axis_index_groups=x_groups).astype(WIDE).sum(0).astype(LOW)
    split = Y_SIZE * own_count
    gram_rows = taken[split + 2 * share :]
    mine = taken[split : split + 2 * share]
    sent = jnp.concatenate(
        [
            taken[:split].reshape(Y_SIZE, own_count, width),
            jnp.broadcast_to(mine, (Y_SIZE,) + mine.shape),
        ],
        axis=1,
    )
    summed = lax.all_to_all(sent, "subj", 0, 0, axis_index_groups=y_groups)
    summed = summed.astype(WIDE).sum(0).astype(LOW)
    own_stats = summed[:own_count]
    other_stats = lax.ppermute(own_stats, "comp", SWAP)
    mine = jnp.concatenate([summed[own_count:], gram_rows], axis=0)
    shared = lax.all_to_all(jnp.broadcast_to(mine, (ring,) + mine.shape), ring_axes, 0, 0)

    gram_at = 2 * share
    low_block, high_block, cross = [
        shared[:, gram_at + i * few : gram_at + (i + 1) * few].reshape(own_count, own_count) for i in range(3)
    ]
    gram = jnp.concatenate(
        [jnp.concatenate([low_block, cross], axis=1), jnp.concatenate([cross.T, high_block], axis=1)], axis=0
    ).astype(WIDE)
    coding = power_sum(gram)
    own_coding = lax.dynamic_slice_in_dim(coding, comp * own_count, own_count, 1)
    product = jnp.transpose(shared[:, :gram_at].reshape(slabs, 2, 2, share, own_count), (1, 0, 3, 2, 4))
    product = product.reshape(COMPONENTS, COMPONENTS).astype(WIDE)
    product = jnp.dot(jnp.dot(own_coding.T, product, precision=highest), coding, precision=highest)
    codes = jnp.dot(proj.astype(WIDE), own_coding, precision=highest)
    both_stats = jnp.where(
        comp == 0,
        jnp.concatenate([own_stats, other_stats], axis=0),
        jnp.concatenate([other_stats, own_stats], axis=0),
    ).astype(WIDE)
    stats_line = 0.5 * stats_old.reshape(own_count, width) + jnp.dot(own_coding.T, both_stats, precision=highest)
    gram_new = 0.5 * gram_old + product
    own_piece = own_line.reshape(own_count, width)
    other_piece = got[:, part]
    piece = jnp.where(
        comp == 0,
        jnp.concatenate([own_piece, other_piece], axis=0),
        jnp.concatenate([other_piece, own_piece], axis=0),
    ).astype(WIDE)
    block = lax.dynamic_slice_in_dim(gram_new, comp * own_count, own_count, 1)
    diag = jnp.sum(block * jnp.eye(own_count, dtype=WIDE), axis=1, keepdims=True)
    coupled = jnp.dot(gram_new, piece, precision=highest)
    updated = own_piece.astype(WIDE) + (stats_line - coupled) / diag
    edge = updated.astype(LOW)
    sides = []
    for axis in ("slab", "subj"):
        count = lax.axis_size(axis)
        up = [(i, i + 1) for i in range(count - 1)]
        sides.append(lax.ppermute(edge, axis, up) + 0.0)
        sides.append(lax.ppermute(edge, axis, [(b, a) for a, b in up]) + 0.0)
    z_low, z_high, y_low, y_high = [side.astype(WIDE) for side in sides]
    side_x = jnp.pad(updated, ((0, 0), (1, 1)))
    lap_x = side_x[:, 2:] + side_x[:, :-2] - 2.0 * updated
    lap_z = z_low + z_high - 2.0 * updated
    lap_y = y_low + y_high - 2.0 * updated
    maps_new = (updated + 0.24 * lap_z + 0.18 * lap_y + 0.12 * lap_x).astype(LOW)
    return (
        maps_new.reshape(own_count, 1, 1, width),
        stats_line.reshape(own_count, 1, 1, width),
        gram_new,
        codes,
    )


def solution(mesh):
    in_specs = (
        P("subj", "slab", None, None),
        P("comp", "slab", None, None),
        P("comp", None),
        P("comp", "slab", "subj", None),
        P("subj"),
    )
    out_specs = (
        P("comp", "slab", "subj", None),
        P("comp", "slab", "subj", None),
        P("comp", None),
        P("subj", "comp"),
    )
    return jax.shard_map(
        on_device, mesh=mesh, in_specs=in_specs, out_specs=out_specs, check_vma=False
    )
```

```python
import math

import jax
import jax.numpy as jnp
from jax import lax
from jax.sharding import PartitionSpec as P

COMPONENTS = 256
ITERS = 12
X_SIZE = 4
Y_SIZE = 8
LOW = jnp.bfloat16
WIDE = jnp.float32
SWAP = [(0, 1), (1, 0)]


def power_sum(gram):
    dot = lambda a, b: jnp.dot(a, b, precision=lax.Precision.HIGH)
    eye = jnp.eye(COMPONENTS, dtype=WIDE)
    first = 0.98 * eye - 0.1 * gram
    second = dot(first, first)
    third = dot(second, first)
    sum3 = eye + first + second
    sum6 = sum3 + dot(third, sum3)
    sixth = dot(third, third)
    return 0.1 * (sum6 + dot(sixth, sum6))


def on_device(scans, maps, gram_old, stats_old, kept):
    fine = lax.Precision.HIGH
    slabs = lax.axis_size("slab")
    subjects = lax.axis_size("subj")
    volumes = scans.shape[0]
    own_count, _, lines, width = maps.shape
    voxel_total = slabs * lines * width
    total_rows = volumes * subjects
    slab, subj, comp = lax.axis_index("slab"), lax.axis_index("subj"), lax.axis_index("comp")
    ring = slabs * 2
    ring_axes = ("slab", "comp")
    x_groups = [[x * Y_SIZE + y for x in range(X_SIZE)] for y in range(Y_SIZE)]
    y_groups = [[x * Y_SIZE + y for y in range(Y_SIZE)] for x in range(X_SIZE)]

    scans3 = scans.reshape(volumes, lines, width)
    maps3 = maps.reshape(own_count, lines, width)
    own_piece = lax.dynamic_slice_in_dim(maps3, subj, 1, 1).reshape(own_count, width)
    proj_part = jnp.einsum("ryx,kyx->rk", scans3, maps3, preferred_element_type=WIDE)
    proj_part = (proj_part * (1.0 / math.sqrt(voxel_total))).astype(LOW)

    rows = 32
    pieces = volumes // rows
    few = own_count // ring
    sent = jnp.pad(proj_part.reshape(pieces, rows, own_count), ((0, ring - pieces), (0, 0), (0, 0)))
    sent = jnp.concatenate([sent, own_piece.T.reshape(ring, few, own_count)], axis=1)
    taken = lax.all_to_all(sent, ring_axes, 0, 0)
    proj_rows = taken[:, :rows].reshape(slabs, 2, rows, own_count).astype(WIDE).sum(0).astype(LOW)
    voxels = taken[:, rows:].reshape(slabs, 2, few, own_count)
    low_part, high_part = [voxels[:, i].reshape(slabs * few, own_count) for i in range(2)]
    gram_parts = [
        jnp.dot(one.T, two, preferred_element_type=WIDE).reshape(ring, few, own_count)
        for one, two in ((low_part, low_part), (high_part, high_part), (low_part, high_part))
    ]
    gram_parts = (jnp.concatenate(gram_parts, axis=1) * (1.0 / voxel_total)).astype(LOW)
    proj_rows = jnp.broadcast_to(proj_rows.reshape(2 * rows, own_count), (ring, 2 * rows, own_count))
    back = lax.all_to_all(jnp.concatenate([proj_rows, gram_parts], axis=1), ring_axes, 0, 0)
    proj_pair = [back[:pieces, i * rows : (i + 1) * rows].reshape(volumes, own_count) for i in range(2)]
    proj = jnp.concatenate(proj_pair, axis=1)
    gram_rows = back[:, 2 * rows :].astype(WIDE).sum(0).astype(LOW)

    live = (lax.iota(jnp.int32, volumes) < kept[0]).astype(LOW)
    live_proj = jnp.where(comp == 0, proj_pair[0], proj_pair[1]) * live[:, None]
    term = jnp.einsum("rk,ryx->ykx", live_proj, scans3, preferred_element_type=WIDE)
    term = (term * (0.5 / math.sqrt(total_rows))).astype(LOW).reshape(X_SIZE, Y_SIZE * own_count, width)
    product = jnp.dot(live_proj.T, proj, preferred_element_type=WIDE) * (0.5 / total_rows)
    share = own_count // slabs
    mine = lax.dynamic_slice_in_dim(product, slab * share, share, 0).astype(LOW)
    mine = jnp.concatenate([mine[:, :own_count], mine[:, own_count:], gram_rows], axis=0)
    sent = jnp.concatenate([term, jnp.broadcast_to(mine, (X_SIZE,) + mine.shape)], axis=1)
    taken = lax.all_to_all(sent, "subj", 0, 0, axis_index_groups=x_groups).astype(WIDE).sum(0).astype(LOW)
    split = Y_SIZE * own_count
    mine = taken[split:]
    sent = jnp.concatenate(
        [
            taken[:split].reshape(Y_SIZE, own_count, width),
            jnp.broadcast_to(mine, (Y_SIZE,) + mine.shape),
        ],
        axis=1,
    )
    summed = lax.all_to_all(sent, "subj", 0, 0, axis_index_groups=y_groups)
    summed = summed.astype(WIDE).sum(0).astype(LOW)
    own_stats = summed[:own_count]
    other = lax.ppermute(jnp.concatenate([own_stats, own_piece], axis=0), "comp", SWAP)
    other_stats, other_piece = other[:own_count], other[own_count:]
    mine = summed[own_count:]
    shared = lax.all_to_all(jnp.broadcast_to(mine, (ring,) + mine.shape), ring_axes, 0, 0)

    gram_at = 2 * share
    low_block, high_block, cross = [
        shared[:, gram_at + i * few : gram_at + (i + 1) * few].reshape(own_count, own_count) for i in range(3)
    ]
    gram = jnp.concatenate(
        [jnp.concatenate([low_block, cross], axis=1), jnp.concatenate([cross.T, high_block], axis=1)], axis=0
    ).astype(WIDE)
    coding = power_sum(gram)
    own_coding = lax.dynamic_slice_in_dim(coding, comp * own_count, own_count, 1)
    product = jnp.transpose(shared[:, :gram_at].reshape(slabs, 2, 2, share, own_count), (1, 0, 3, 2, 4))
    product = product.reshape(COMPONENTS, COMPONENTS).astype(WIDE)
    product = jnp.dot(jnp.dot(own_coding.T, product, precision=fine), coding, precision=fine)
    codes = jnp.dot(proj.astype(WIDE), own_coding, precision=fine)
    both_stats = jnp.where(
        comp == 0,
        jnp.concatenate([own_stats, other_stats], axis=0),
        jnp.concatenate([other_stats, own_stats], axis=0),
    ).astype(WIDE)
    stats_line = 0.5 * stats_old.reshape(own_count, width) + jnp.dot(own_coding.T, both_stats, precision=fine)
    gram_new = 0.5 * gram_old + product
    piece = jnp.where(
        comp == 0,
        jnp.concatenate([own_piece, other_piece], axis=0),
        jnp.concatenate([other_piece, own_piece], axis=0),
    ).astype(WIDE)
    block = lax.dynamic_slice_in_dim(gram_new, comp * own_count, own_count, 1)
    diag = jnp.sum(block * jnp.eye(own_count, dtype=WIDE), axis=1, keepdims=True)
    coupled = jnp.dot(gram_new, piece, precision=fine)
    updated = own_piece.astype(WIDE) + (stats_line - coupled) / diag
    edge = updated.astype(LOW)
    sides = []
    for axis in ("slab", "subj"):
        count = lax.axis_size(axis)
        up = [(i, i + 1) for i in range(count - 1)]
        sides.append(lax.ppermute(edge, axis, up) + 0.0)
        sides.append(lax.ppermute(edge, axis, [(b, a) for a, b in up]) + 0.0)
    z_low, z_high, y_low, y_high = [side.astype(WIDE) for side in sides]
    side_x = jnp.pad(updated, ((0, 0), (1, 1)))
    lap_x = side_x[:, 2:] + side_x[:, :-2] - 2.0 * updated
    lap_z = z_low + z_high - 2.0 * updated
    lap_y = y_low + y_high - 2.0 * updated
    maps_new = (updated + 0.24 * lap_z + 0.18 * lap_y + 0.12 * lap_x).astype(LOW)
    return (
        maps_new.reshape(own_count, 1, 1, width),
        stats_line.reshape(own_count, 1, 1, width),
        gram_new,
        codes,
    )


def solution(mesh):
    in_specs = (
        P("subj", "slab", None, None),
        P("comp", "slab", None, None),
        P("comp", None),
        P("comp", "slab", "subj", None),
        P("subj"),
    )
    out_specs = (
        P("comp", "slab", "subj", None),
        P("comp", "slab", "subj", None),
        P("comp", None),
        P("subj", "comp"),
    )
    return jax.shard_map(
        on_device, mesh=mesh, in_specs=in_specs, out_specs=out_specs, check_vma=False
    )
```

```python
import math

import jax
import jax.numpy as jnp
from jax import lax
from jax.experimental import pallas as pl
from jax.experimental.pallas import tpu as pltpu
from jax.sharding import PartitionSpec as P

COMPONENTS = 256
ITERS = 12
X_SIZE = 4
Y_SIZE = 8
LOW = jnp.bfloat16
WIDE = jnp.float32
SWAP = [(0, 1), (1, 0)]


def power_sum(gram):
    dot = lambda a, b: jnp.dot(a, b, precision=lax.Precision.HIGH)
    eye = jnp.eye(COMPONENTS, dtype=WIDE)
    first = 0.98 * eye - 0.1 * gram
    second = dot(first, first)
    third = dot(second, first)
    sum3 = eye + first + second
    sum6 = sum3 + dot(third, sum3)
    sixth = dot(third, third)
    return 0.1 * (sum6 + dot(sixth, sum6))


def keep_near(array):
    def copy(source, target, sem):
        moved = pltpu.make_async_copy(source, target, sem)
        moved.start()
        moved.wait()

    return pl.pallas_call(
        copy,
        out_shape=pltpu.VMEM(array.shape, array.dtype),
        in_specs=[pl.BlockSpec(memory_space=pltpu.HBM)],
        out_specs=pl.BlockSpec(memory_space=pltpu.VMEM),
        scratch_shapes=[pltpu.SemaphoreType.DMA(())],
        compiler_params=pltpu.CompilerParams(vmem_limit_bytes=1 << 20),
        cost_estimate=pl.CostEstimate(flops=0, bytes_accessed=2 * array.size * 2, transcendentals=0),
    )(array)


def on_device(scans, maps, gram_old, stats_old, kept):
    fine = lax.Precision.HIGH
    slabs = lax.axis_size("slab")
    subjects = lax.axis_size("subj")
    volumes = scans.shape[0]
    own_count, _, lines, width = maps.shape
    voxel_total = slabs * lines * width
    total_rows = volumes * subjects
    slab, subj, comp = lax.axis_index("slab"), lax.axis_index("subj"), lax.axis_index("comp")
    ring = slabs * 2
    ring_axes = ("slab", "comp")
    x_groups = [[x * Y_SIZE + y for x in range(X_SIZE)] for y in range(Y_SIZE)]
    y_groups = [[x * Y_SIZE + y for y in range(Y_SIZE)] for x in range(X_SIZE)]

    scans3 = keep_near(scans.reshape(volumes, lines, width))
    maps3 = maps.reshape(own_count, lines, width)
    own_piece = lax.dynamic_slice_in_dim(maps3, subj, 1, 1).reshape(own_count, width)
    proj_part = jnp.einsum("ryx,kyx->rk", scans3, maps3, preferred_element_type=WIDE)
    proj_part = (proj_part * (1.0 / math.sqrt(voxel_total))).astype(LOW)

    rows = 32
    pieces = volumes // rows
    few = own_count // ring
    sent = jnp.pad(proj_part.reshape(pieces, rows, own_count), ((0, ring - pieces), (0, 0), (0, 0)))
    sent = jnp.concatenate([sent, own_piece.T.reshape(ring, few, own_count)], axis=1)
    taken = lax.all_to_all(sent, ring_axes, 0, 0)
    proj_rows = taken[:, :rows].reshape(slabs, 2, rows, own_count).astype(WIDE).sum(0).astype(LOW)
    voxels = taken[:, rows:].reshape(slabs, 2, few, own_count)
    low_part, high_part = [voxels[:, i].reshape(slabs * few, own_count) for i in range(2)]
    gram_parts = [
        jnp.dot(one.T, two, preferred_element_type=WIDE).reshape(ring, few, own_count)
        for one, two in ((low_part, low_part), (high_part, high_part), (low_part, high_part))
    ]
    gram_parts = (jnp.concatenate(gram_parts, axis=1) * (1.0 / voxel_total)).astype(LOW)
    proj_rows = jnp.broadcast_to(proj_rows.reshape(2 * rows, own_count), (ring, 2 * rows, own_count))
    back = lax.all_to_all(jnp.concatenate([proj_rows, gram_parts], axis=1), ring_axes, 0, 0)
    proj_pair = [back[:pieces, i * rows : (i + 1) * rows].reshape(volumes, own_count) for i in range(2)]
    proj = jnp.concatenate(proj_pair, axis=1)
    gram_rows = back[:, 2 * rows :].astype(WIDE).sum(0).astype(LOW)

    live = (lax.iota(jnp.int32, volumes) < kept[0]).astype(LOW)
    live_proj = jnp.where(comp == 0, proj_pair[0], proj_pair[1]) * live[:, None]
    term = jnp.einsum("rk,ryx->ykx", live_proj, scans3, preferred_element_type=WIDE)
    term = (term * (0.5 / math.sqrt(total_rows))).astype(LOW).reshape(X_SIZE, Y_SIZE * own_count, width)
    product = jnp.dot(live_proj.T, proj, preferred_element_type=WIDE) * (0.5 / total_rows)
    share = own_count // slabs
    mine = lax.dynamic_slice_in_dim(product, slab * share, share, 0).astype(LOW)
    mine = jnp.concatenate([mine[:, :own_count], mine[:, own_count:], gram_rows], axis=0)
    sent = jnp.concatenate([term, jnp.broadcast_to(mine, (X_SIZE,) + mine.shape)], axis=1)
    taken = lax.all_to_all(sent, "subj", 0, 0, axis_index_groups=x_groups).astype(WIDE).sum(0).astype(LOW)
    split = Y_SIZE * own_count
    mine = taken[split:]
    sent = jnp.concatenate(
        [
            taken[:split].reshape(Y_SIZE, own_count, width),
            jnp.broadcast_to(mine, (Y_SIZE,) + mine.shape),
        ],
        axis=1,
    )
    summed = lax.all_to_all(sent, "subj", 0, 0, axis_index_groups=y_groups)
    summed = summed.astype(WIDE).sum(0).astype(LOW)
    own_stats = summed[:own_count]
    other = lax.ppermute(jnp.concatenate([own_stats, own_piece], axis=0), "comp", SWAP)
    other_stats, other_piece = other[:own_count], other[own_count:]
    mine = summed[own_count:]
    shared = lax.all_to_all(jnp.broadcast_to(mine, (ring,) + mine.shape), ring_axes, 0, 0)

    gram_at = 2 * share
    low_block, high_block, cross = [
        shared[:, gram_at + i * few : gram_at + (i + 1) * few].reshape(own_count, own_count) for i in range(3)
    ]
    gram = jnp.concatenate(
        [jnp.concatenate([low_block, cross], axis=1), jnp.concatenate([cross.T, high_block], axis=1)], axis=0
    ).astype(WIDE)
    coding = power_sum(gram)
    own_coding = lax.dynamic_slice_in_dim(coding, comp * own_count, own_count, 1)
    product = jnp.transpose(shared[:, :gram_at].reshape(slabs, 2, 2, share, own_count), (1, 0, 3, 2, 4))
    product = product.reshape(COMPONENTS, COMPONENTS).astype(WIDE)
    product = jnp.dot(jnp.dot(own_coding.T, product, precision=fine), coding, precision=fine)
    codes = jnp.dot(proj.astype(WIDE), own_coding, precision=fine)
    both_stats = jnp.where(
        comp == 0,
        jnp.concatenate([own_stats, other_stats], axis=0),
        jnp.concatenate([other_stats, own_stats], axis=0),
    ).astype(WIDE)
    stats_line = 0.5 * stats_old.reshape(own_count, width) + jnp.dot(own_coding.T, both_stats, precision=fine)
    gram_new = 0.5 * gram_old + product
    piece = jnp.where(
        comp == 0,
        jnp.concatenate([own_piece, other_piece], axis=0),
        jnp.concatenate([other_piece, own_piece], axis=0),
    ).astype(WIDE)
    block = lax.dynamic_slice_in_dim(gram_new, comp * own_count, own_count, 1)
    diag = jnp.sum(block * jnp.eye(own_count, dtype=WIDE), axis=1, keepdims=True)
    coupled = jnp.dot(gram_new, piece, precision=fine)
    updated = own_piece.astype(WIDE) + (stats_line - coupled) / diag
    edge = updated.astype(LOW)
    sides = []
    for axis in ("slab", "subj"):
        count = lax.axis_size(axis)
        up = [(i, i + 1) for i in range(count - 1)]
        sides.append(lax.ppermute(edge, axis, up) + 0.0)
        sides.append(lax.ppermute(edge, axis, [(b, a) for a, b in up]) + 0.0)
    z_low, z_high, y_low, y_high = [side.astype(WIDE) for side in sides]
    side_x = jnp.pad(updated, ((0, 0), (1, 1)))
    lap_x = side_x[:, 2:] + side_x[:, :-2] - 2.0 * updated
    lap_z = z_low + z_high - 2.0 * updated
    lap_y = y_low + y_high - 2.0 * updated
    maps_new = (updated + 0.24 * lap_z + 0.18 * lap_y + 0.12 * lap_x).astype(LOW)
    return (
        maps_new.reshape(own_count, 1, 1, width),
        stats_line.reshape(own_count, 1, 1, width),
        gram_new,
        codes,
    )


def solution(mesh):
    in_specs = (
        P("subj", "slab", None, None),
        P("comp", "slab", None, None),
        P("comp", None),
        P("comp", "slab", "subj", None),
        P("subj"),
    )
    out_specs = (
        P("comp", "slab", "subj", None),
        P("comp", "slab", "subj", None),
        P("comp", None),
        P("subj", "comp"),
    )
    return jax.shard_map(
        on_device, mesh=mesh, in_specs=in_specs, out_specs=out_specs, check_vma=False
    )
```

```python
import math

import jax
import jax.numpy as jnp
from jax import lax
from jax.sharding import PartitionSpec as P

COMPONENTS = 256
ITERS = 12
X_SIZE = 4
Y_SIZE = 8
LOW = jnp.bfloat16
WIDE = jnp.float32
SWAP = [(0, 1), (1, 0)]


def power_sum(gram):
    dot = lambda a, b: jnp.dot(a, b, precision=lax.Precision.HIGH)
    eye = jnp.eye(COMPONENTS, dtype=WIDE)
    first = 0.98 * eye - 0.1 * gram
    second = dot(first, first)
    third = dot(second, first)
    sum3 = eye + first + second
    sum6 = sum3 + dot(third, sum3)
    sixth = dot(third, third)
    return 0.1 * (sum6 + dot(sixth, sum6))


def symmetric(low, cross, high):
    top = jnp.concatenate([low, cross], axis=1)
    return jnp.concatenate([top, jnp.concatenate([cross.T, high], axis=1)], axis=0).astype(WIDE)


def on_device(scans, maps, gram_old, stats_old, kept):
    fine = lax.Precision.HIGH
    slabs = lax.axis_size("slab")
    subjects = lax.axis_size("subj")
    volumes = scans.shape[0]
    own_count, _, lines, width = maps.shape
    voxel_total = slabs * lines * width
    total_rows = volumes * subjects
    slab, subj, comp = lax.axis_index("slab"), lax.axis_index("subj"), lax.axis_index("comp")
    ring = slabs * 2
    ring_axes = ("slab", "comp")
    x_groups = [[x * Y_SIZE + y for x in range(X_SIZE)] for y in range(Y_SIZE)]
    y_groups = [[x * Y_SIZE + y for y in range(Y_SIZE)] for x in range(X_SIZE)]

    scans3 = scans.reshape(volumes, lines, width)
    maps3 = maps.reshape(own_count, lines, width)
    own_piece = lax.dynamic_slice_in_dim(maps3, subj, 1, 1).reshape(own_count, width)
    proj_part = jnp.einsum("ryx,kyx->rk", scans3, maps3, preferred_element_type=WIDE)
    proj_part = (proj_part * (1.0 / math.sqrt(voxel_total))).astype(LOW)

    rows = 32
    pieces = volumes // rows
    few = own_count // ring
    sent = jnp.pad(proj_part.reshape(pieces, rows, own_count), ((0, ring - pieces), (0, 0), (0, 0)))
    sent = jnp.concatenate([sent, own_piece.T.reshape(ring, few, own_count)], axis=1)
    taken = lax.all_to_all(sent, ring_axes, 0, 0)
    proj_rows = taken[:, :rows].reshape(slabs, 2, rows, own_count).astype(WIDE).sum(0).astype(LOW)
    voxels = taken[:, rows:].reshape(slabs, 2, few, own_count)
    low_part, high_part = [voxels[:, i].reshape(slabs * few, own_count) for i in range(2)]
    shares = [
        jnp.dot(one.T, two, preferred_element_type=WIDE) * (1.0 / voxel_total)
        for one, two in ((low_part, low_part), (high_part, high_part), (low_part, high_part))
    ]
    product_scale = 0.5 / total_rows
    first_row = (2 * slab + comp) * rows
    live = (first_row + lax.iota(jnp.int32, rows) < kept[0]).astype(LOW)
    shares.append(
        jnp.dot((proj_rows[0] * live[:, None]).T, proj_rows[1], preferred_element_type=WIDE) * product_scale
    )
    shares = jnp.concatenate([share.reshape(ring, few, own_count) for share in shares], axis=1).astype(LOW)
    to_owner = jnp.broadcast_to(proj_rows, (slabs, 2, rows, own_count)).reshape(ring, rows, own_count)
    back = lax.all_to_all(jnp.concatenate([to_owner, shares], axis=1), ring_axes, 0, 0)
    proj_own = back[:pieces, :rows].reshape(volumes, own_count)
    shares = back[:, rows:].astype(WIDE).sum(0).astype(LOW)

    live = (lax.iota(jnp.int32, volumes) < kept[0]).astype(LOW)
    live_proj = proj_own * live[:, None]
    term = jnp.einsum("rk,ryx->ykx", live_proj, scans3, preferred_element_type=WIDE)
    term = (term * (0.5 / math.sqrt(total_rows))).astype(LOW).reshape(X_SIZE, Y_SIZE * own_count, width)
    product = jnp.dot(live_proj.T, proj_own, preferred_element_type=WIDE) * product_scale
    square = own_count // slabs
    mine = lax.dynamic_slice_in_dim(product, slab * square, square, 0).astype(LOW)
    mine = jnp.concatenate([mine, shares], axis=0)
    sent = jnp.concatenate([term, jnp.broadcast_to(mine, (X_SIZE,) + mine.shape)], axis=1)
    taken = lax.all_to_all(sent, "subj", 0, 0, axis_index_groups=x_groups).astype(WIDE).sum(0).astype(LOW)
    split = Y_SIZE * own_count
    mine = taken[split:]
    sent = jnp.concatenate(
        [
            taken[:split].reshape(Y_SIZE, own_count, width),
            jnp.broadcast_to(mine, (Y_SIZE,) + mine.shape),
        ],
        axis=1,
    )
    summed = lax.all_to_all(sent, "subj", 0, 0, axis_index_groups=y_groups)
    summed = summed.astype(WIDE).sum(0).astype(LOW)
    own_stats = summed[:own_count]
    other = lax.ppermute(jnp.concatenate([own_stats, own_piece], axis=0), "comp", SWAP)
    other_stats, other_piece = other[:own_count], other[own_count:]
    mine = jnp.broadcast_to(summed[own_count:], (slabs, 2, square + 4 * few, own_count))
    to_other = jnp.broadcast_to(proj_rows[::-1], (slabs, 2, rows, own_count))
    shared = jnp.concatenate([mine, to_other], axis=2).reshape(ring, -1, own_count)
    shared = lax.all_to_all(shared, ring_axes, 0, 0)

    squares = shared[:, :square].reshape(slabs, 2, square, own_count)
    low_block, high_block, cross, product_cross = [
        shared[:, square + i * few : square + (i + 1) * few].reshape(own_count, own_count) for i in range(4)
    ]
    proj_other = shared[:pieces, square + 4 * few :].reshape(volumes, own_count)
    gram = symmetric(low_block, cross, high_block)
    product = symmetric(squares[:, 0].reshape(own_count, own_count), product_cross, squares[:, 1].reshape(own_count, own_count))
    coding = power_sum(gram)
    own_coding = lax.dynamic_slice_in_dim(coding, comp * own_count, own_count, 1)
    product = jnp.dot(jnp.dot(own_coding.T, product, precision=fine), coding, precision=fine)
    from_own = lax.dynamic_slice_in_dim(own_coding, comp * own_count, own_count, 0)
    from_other = lax.dynamic_slice_in_dim(own_coding, (1 - comp) * own_count, own_count, 0)
    codes = jnp.dot(proj_own.astype(WIDE), from_own, precision=fine)
    codes = codes + jnp.dot(proj_other.astype(WIDE), from_other, precision=fine)
    added = jnp.dot(from_own.T, own_stats.astype(WIDE), precision=fine)
    added = added + jnp.dot(from_other.T, other_stats.astype(WIDE), precision=fine)
    stats_line = 0.5 * stats_old.reshape(own_count, width) + added
    gram_new = 0.5 * gram_old + product
    block = lax.dynamic_slice_in_dim(gram_new, comp * own_count, own_count, 1)
    other_block = lax.dynamic_slice_in_dim(gram_new, (1 - comp) * own_count, own_count, 1)
    diag = jnp.sum(block * jnp.eye(own_count, dtype=WIDE), axis=1, keepdims=True)
    coupled = jnp.dot(block, own_piece.astype(WIDE), precision=fine)
    coupled = coupled + jnp.dot(other_block, other_piece.astype(WIDE), precision=fine)
    updated = own_piece.astype(WIDE) + (stats_line - coupled) / diag
    edge = updated.astype(LOW)
    sides = []
    for axis in ("slab", "subj"):
        count = lax.axis_size(axis)
        up = [(i, i + 1) for i in range(count - 1)]
        sides.append(lax.ppermute(edge, axis, up) + 0.0)
        sides.append(lax.ppermute(edge, axis, [(b, a) for a, b in up]) + 0.0)
    z_low, z_high, y_low, y_high = [side.astype(WIDE) for side in sides]
    side_x = jnp.pad(updated, ((0, 0), (1, 1)))
    lap_x = side_x[:, 2:] + side_x[:, :-2] - 2.0 * updated
    lap_z = z_low + z_high - 2.0 * updated
    lap_y = y_low + y_high - 2.0 * updated
    maps_new = (updated + 0.24 * lap_z + 0.18 * lap_y + 0.12 * lap_x).astype(LOW)
    return (
        maps_new.reshape(own_count, 1, 1, width),
        stats_line.reshape(own_count, 1, 1, width),
        gram_new,
        codes,
    )


def solution(mesh):
    in_specs = (
        P("subj", "slab", None, None),
        P("comp", "slab", None, None),
        P("comp", None),
        P("comp", "slab", "subj", None),
        P("subj"),
    )
    out_specs = (
        P("comp", "slab", "subj", None),
        P("comp", "slab", "subj", None),
        P("comp", None),
        P("subj", "comp"),
    )
    return jax.shard_map(
        on_device, mesh=mesh, in_specs=in_specs, out_specs=out_specs, check_vma=False
    )
```

```python
import math

import jax
import jax.numpy as jnp
from jax import lax
from jax.sharding import PartitionSpec as P

COMPONENTS = 256
ITERS = 12
X_SIZE = 4
Y_SIZE = 8
LOW = jnp.bfloat16
WIDE = jnp.float32
SWAP = [(0, 1), (1, 0)]


def power_sum(gram):
    dot = lambda a, b: jnp.dot(a, b, precision=lax.Precision.HIGH)
    eye = jnp.eye(COMPONENTS, dtype=WIDE)
    first = 0.98 * eye - 0.1 * gram
    second = dot(first, first)
    third = dot(second, first)
    sum3 = eye + first + second
    sum6 = sum3 + dot(third, sum3)
    sixth = dot(third, third)
    return 0.1 * (sum6 + dot(sixth, sum6))


def after(value, done):
    return value + (done != done).astype(value.dtype)


def symmetric(low, cross, high):
    top = jnp.concatenate([low, cross], axis=1)
    return jnp.concatenate([top, jnp.concatenate([cross.T, high], axis=1)], axis=0).astype(WIDE)


def on_device(scans, maps, gram_old, stats_old, kept):
    fine = lax.Precision.HIGH
    slabs = lax.axis_size("slab")
    subjects = lax.axis_size("subj")
    volumes = scans.shape[0]
    own_count, _, lines, width = maps.shape
    voxel_total = slabs * lines * width
    total_rows = volumes * subjects
    slab, subj, comp = lax.axis_index("slab"), lax.axis_index("subj"), lax.axis_index("comp")
    ring = slabs * 2
    ring_axes = ("slab", "comp")
    x_groups = [[x * Y_SIZE + y for x in range(X_SIZE)] for y in range(Y_SIZE)]
    y_groups = [[x * Y_SIZE + y for y in range(Y_SIZE)] for x in range(X_SIZE)]

    scans3 = scans.reshape(volumes, lines, width)
    maps3 = maps.reshape(own_count, lines, width)
    own_piece = lax.dynamic_slice_in_dim(maps3, subj, 1, 1).reshape(own_count, width)
    proj_part = jnp.einsum("ryx,kyx->rk", scans3, maps3, preferred_element_type=WIDE)
    proj_part = (proj_part * (1.0 / math.sqrt(voxel_total))).astype(LOW)

    rows = 32
    pieces = volumes // rows
    few = own_count // ring
    square = own_count // slabs
    first_row = (2 * slab + comp) * rows
    first_square = (slab * square).astype(jnp.uint32)
    noted = kept[0] + first_row + first_square.astype(jnp.int32)
    empty = jnp.broadcast_to(noted.astype(LOW), (ring - pieces, rows, own_count))
    sent = jnp.concatenate([proj_part.reshape(pieces, rows, own_count), empty], axis=0)
    sent = jnp.concatenate([sent, own_piece.T.reshape(ring, few, own_count)], axis=1)
    taken = lax.all_to_all(sent, ring_axes, 0, 0)
    proj_rows = taken[:, :rows].reshape(slabs, 2, rows, own_count).astype(WIDE).sum(0).astype(LOW)
    voxels = taken[:, rows:].reshape(slabs, 2, few, own_count)
    voxels = jnp.concatenate([voxels[:, i].reshape(slabs * few, own_count) for i in range(2)], axis=1)
    gram_part = jnp.dot(voxels.T, voxels, preferred_element_type=WIDE) * (1.0 / voxel_total)
    product_scale = 0.5 / total_rows
    at_row = after(lax.broadcasted_iota(jnp.int32, (rows, own_count), 0), proj_rows[0])
    live = first_row + at_row < kept[0]
    cross_part = jnp.dot(jnp.where(live, proj_rows[0], 0).T, proj_rows[1], preferred_element_type=WIDE)
    shares = [gram_part[:own_count, :own_count], gram_part[own_count:, own_count:], gram_part[:own_count, own_count:]]
    shares.append(cross_part * product_scale)
    shares = jnp.stack(shares).astype(LOW).reshape(4, ring, few, own_count)
    shares = jnp.transpose(shares, (1, 0, 2, 3)).reshape(ring, 4 * few, own_count)
    to_owner = jnp.broadcast_to(proj_rows, (slabs, 2, rows, own_count)).reshape(ring, rows, own_count)
    back = lax.all_to_all(jnp.concatenate([to_owner, shares], axis=1), ring_axes, 0, 0)
    proj_own = back[:pieces, :rows]
    at_piece = after(lax.broadcasted_iota(jnp.int32, proj_own.shape, 0), proj_own)
    left = kept[0] - rows * at_piece
    live_proj = jnp.where(lax.broadcasted_iota(jnp.int32, proj_own.shape, 1) < left, proj_own, 0).reshape(volumes, own_count)
    proj_own = proj_own.reshape(volumes, own_count)
    shares = back[:, rows:].astype(WIDE).sum(0).astype(LOW)
    term = jnp.einsum("rk,ryx->ykx", live_proj, scans3, preferred_element_type=WIDE)
    term = (term * (0.5 / math.sqrt(total_rows))).astype(LOW).reshape(X_SIZE, Y_SIZE * own_count, width)
    product = jnp.dot(live_proj.T, proj_own, preferred_element_type=WIDE) * product_scale
    mine = lax.dynamic_slice(product, (first_square, jnp.uint32(0)), (square, own_count)).astype(LOW)
    mine = jnp.concatenate([mine, shares], axis=0)
    sent = jnp.concatenate([term, jnp.broadcast_to(mine, (X_SIZE,) + mine.shape)], axis=1)
    taken = lax.all_to_all(sent, "subj", 0, 0, axis_index_groups=x_groups).astype(WIDE).sum(0).astype(LOW)
    split = Y_SIZE * own_count
    mine = taken[split:]
    sent = jnp.concatenate(
        [
            taken[:split].reshape(Y_SIZE, own_count, width),
            jnp.broadcast_to(mine, (Y_SIZE,) + mine.shape),
        ],
        axis=1,
    )
    summed = lax.all_to_all(sent, "subj", 0, 0, axis_index_groups=y_groups)
    summed = summed.astype(WIDE).sum(0).astype(LOW)
    own_stats = summed[:own_count]
    other = lax.ppermute(jnp.concatenate([own_stats, own_piece], axis=0), "comp", SWAP)
    other_stats, other_piece = other[:own_count], other[own_count:]
    mine = summed[own_count:]
    late_rows = after(proj_rows, mine[:rows])
    shared = jnp.concatenate([mine, late_rows[1], mine, late_rows[0]], axis=0).reshape(2, -1, own_count)
    shared = jnp.broadcast_to(shared, (slabs,) + shared.shape).reshape(ring, -1, own_count)
    shared = lax.all_to_all(shared, ring_axes, 0, 0)

    squares = shared[:, :square].reshape(slabs, 2, square, own_count)
    low_block, high_block, cross, product_cross = [
        shared[:, square + i * few : square + (i + 1) * few].reshape(own_count, own_count) for i in range(4)
    ]
    proj_other = shared[:pieces, square + 4 * few :].reshape(volumes, own_count)
    gram = symmetric(low_block, cross, high_block)
    product = symmetric(squares[:, 0].reshape(own_count, own_count), product_cross, squares[:, 1].reshape(own_count, own_count))
    coding = power_sum(gram)
    own_coding = lax.dynamic_slice_in_dim(coding, comp * own_count, own_count, 1)
    product = jnp.dot(jnp.dot(own_coding.T, product, precision=fine), coding, precision=fine)
    from_own = lax.dynamic_slice_in_dim(own_coding, comp * own_count, own_count, 0)
    from_other = lax.dynamic_slice_in_dim(own_coding, (1 - comp) * own_count, own_count, 0)
    codes = jnp.dot(proj_own.astype(WIDE), from_own, precision=fine)
    codes = codes + jnp.dot(proj_other.astype(WIDE), from_other, precision=fine)
    added = jnp.dot(from_own.T, own_stats.astype(WIDE), precision=fine)
    added = added + jnp.dot(from_other.T, other_stats.astype(WIDE), precision=fine)
    stats_line = 0.5 * stats_old.reshape(own_count, width) + added
    gram_new = 0.5 * gram_old + product
    block = lax.dynamic_slice_in_dim(gram_new, comp * own_count, own_count, 1)
    other_block = lax.dynamic_slice_in_dim(gram_new, (1 - comp) * own_count, own_count, 1)
    diag = jnp.sum(block * jnp.eye(own_count, dtype=WIDE), axis=1, keepdims=True)
    coupled = jnp.dot(block, own_piece.astype(WIDE), precision=fine)
    coupled = coupled + jnp.dot(other_block, other_piece.astype(WIDE), precision=fine)
    updated = own_piece.astype(WIDE) + (stats_line - coupled) / diag
    edge = updated.astype(LOW)
    sides = []
    for axis in ("slab", "subj"):
        count = lax.axis_size(axis)
        up = [(i, i + 1) for i in range(count - 1)]
        sides.append(lax.ppermute(edge, axis, up) + 0.0)
        sides.append(lax.ppermute(edge, axis, [(b, a) for a, b in up]) + 0.0)
    z_low, z_high, y_low, y_high = [side.astype(WIDE) for side in sides]
    side_x = jnp.pad(updated, ((0, 0), (1, 1)))
    lap_x = side_x[:, 2:] + side_x[:, :-2] - 2.0 * updated
    lap_z = z_low + z_high - 2.0 * updated
    lap_y = y_low + y_high - 2.0 * updated
    maps_new = (updated + 0.24 * lap_z + 0.18 * lap_y + 0.12 * lap_x).astype(LOW)
    return (
        maps_new.reshape(own_count, 1, 1, width),
        stats_line.reshape(own_count, 1, 1, width),
        gram_new,
        codes,
    )


def solution(mesh):
    in_specs = (
        P("subj", "slab", None, None),
        P("comp", "slab", None, None),
        P("comp", None),
        P("comp", "slab", "subj", None),
        P("subj"),
    )
    out_specs = (
        P("comp", "slab", "subj", None),
        P("comp", "slab", "subj", None),
        P("comp", None),
        P("subj", "comp"),
    )
    return jax.shard_map(
        on_device, mesh=mesh, in_specs=in_specs, out_specs=out_specs, check_vma=False
    )
```

```python
import math

import jax
import jax.numpy as jnp
from jax import lax
from jax.sharding import PartitionSpec as P

COMPONENTS = 256
ITERS = 12
X_SIZE = 4
Y_SIZE = 8
LOW = jnp.bfloat16
WIDE = jnp.float32
SWAP = [(0, 1), (1, 0)]


def power_sum(gram):
    dot = lambda a, b: jnp.dot(a, b, precision=lax.Precision.HIGH)
    eye = jnp.eye(COMPONENTS, dtype=WIDE)
    first = 0.98 * eye - 0.1 * gram
    second = dot(first, first)
    third = dot(second, first)
    sum3 = eye + first + second
    sum6 = sum3 + dot(third, sum3)
    sixth = dot(third, third)
    return 0.1 * (sum6 + dot(sixth, sum6))


def after(value, done):
    return value + (done != done).astype(value.dtype)


def symmetric(low, cross, high):
    top = jnp.concatenate([low, cross], axis=1)
    return jnp.concatenate([top, jnp.concatenate([cross.T, high], axis=1)], axis=0).astype(WIDE)


def on_device(scans, maps, gram_old, stats_old, kept):
    fine = lax.Precision.HIGH
    slabs = lax.axis_size("slab")
    subjects = lax.axis_size("subj")
    volumes = scans.shape[0]
    own_count, _, lines, width = maps.shape
    voxel_total = slabs * lines * width
    total_rows = volumes * subjects
    slab, subj, comp = lax.axis_index("slab"), lax.axis_index("subj"), lax.axis_index("comp")
    ring = slabs * 2
    ring_axes = ("slab", "comp")
    x_groups = [[x * Y_SIZE + y for x in range(X_SIZE)] for y in range(Y_SIZE)]
    y_groups = [[x * Y_SIZE + y for y in range(Y_SIZE)] for x in range(X_SIZE)]

    scans3 = scans.reshape(volumes, lines, width)
    maps3 = maps.reshape(own_count, lines, width)
    own_piece = lax.dynamic_slice_in_dim(maps3, subj, 1, 1).reshape(own_count, width)
    proj_part = jnp.einsum("ryx,kyx->rk", scans3, maps3, preferred_element_type=WIDE)
    proj_part = (proj_part * (1.0 / math.sqrt(voxel_total))).astype(LOW)

    rows = 32
    pieces = volumes // rows
    few = own_count // ring
    square = own_count // slabs
    first_row = (2 * slab + comp) * rows
    first_square = (slab * square).astype(jnp.uint32)
    noted = kept[0] + first_row + first_square.astype(jnp.int32)
    empty = jnp.broadcast_to(noted.astype(LOW), (ring - pieces, rows, own_count))
    sent = jnp.concatenate([proj_part.reshape(pieces, rows, own_count), empty], axis=0)
    sent = jnp.concatenate([sent, after(own_piece.T, proj_part[:width]).reshape(ring, few, own_count)], axis=1)
    taken = lax.all_to_all(sent, ring_axes, 0, 0)
    proj_rows = taken[:, :rows].reshape(slabs, 2, rows, own_count).astype(WIDE).sum(0).astype(LOW)
    voxels = taken[:, rows:].reshape(slabs, 2, few, own_count)
    voxels = jnp.concatenate([voxels[:, i].reshape(slabs * few, own_count) for i in range(2)], axis=1)
    gram_part = jnp.dot(voxels.T, voxels, preferred_element_type=WIDE) * (1.0 / voxel_total)
    product_scale = 0.5 / total_rows
    at_row = after(lax.broadcasted_iota(jnp.int32, (rows, own_count), 0), proj_rows[0])
    live = first_row + at_row < kept[0]
    cross_part = jnp.dot(jnp.where(live, proj_rows[0], 0).T, proj_rows[1], preferred_element_type=WIDE)
    shares = [gram_part[:own_count, :own_count], gram_part[own_count:, own_count:], gram_part[:own_count, own_count:]]
    shares.append(cross_part * product_scale)
    shares = jnp.stack(shares).astype(LOW).reshape(4, ring, few, own_count)
    shares = jnp.transpose(shares, (1, 0, 2, 3)).reshape(ring, 4 * few, own_count)
    to_owner = jnp.broadcast_to(proj_rows, (slabs, 2, rows, own_count)).reshape(ring, rows, own_count)
    back = lax.all_to_all(jnp.concatenate([to_owner, shares], axis=1), ring_axes, 0, 0)
    proj_own = back[:pieces, :rows]
    at_piece = after(lax.broadcasted_iota(jnp.int32, proj_own.shape, 0), proj_own)
    left = kept[0] - rows * at_piece
    live_proj = jnp.where(lax.broadcasted_iota(jnp.int32, proj_own.shape, 1) < left, proj_own, 0).reshape(volumes, own_count)
    proj_own = proj_own.reshape(volumes, own_count)
    shares = back[:, rows:].astype(WIDE).sum(0).astype(LOW)
    term = jnp.einsum("rk,ryx->ykx", live_proj, scans3, preferred_element_type=WIDE)
    term = (term * (0.5 / math.sqrt(total_rows))).astype(LOW).reshape(X_SIZE, Y_SIZE * own_count, width)
    product = jnp.dot(live_proj.T, proj_own, preferred_element_type=WIDE) * product_scale
    mine = lax.dynamic_slice(product, (first_square, jnp.uint32(0)), (square, own_count)).astype(LOW)
    mine = jnp.concatenate([mine, shares], axis=0)
    sent = jnp.concatenate([term, jnp.broadcast_to(mine, (X_SIZE,) + mine.shape)], axis=1)
    taken = lax.all_to_all(sent, "subj", 0, 0, axis_index_groups=x_groups).astype(WIDE).sum(0).astype(LOW)
    split = Y_SIZE * own_count
    mine = taken[split:]
    sent = jnp.concatenate(
        [
            taken[:split].reshape(Y_SIZE, own_count, width),
            jnp.broadcast_to(mine, (Y_SIZE,) + mine.shape),
        ],
        axis=1,
    )
    summed = lax.all_to_all(sent, "subj", 0, 0, axis_index_groups=y_groups)
    summed = summed.astype(WIDE).sum(0).astype(LOW)
    own_stats = summed[:own_count]
    other = lax.ppermute(jnp.concatenate([own_stats, own_piece], axis=0), "comp", SWAP)
    both_stats, both_piece = [
        jnp.where(comp == 0, jnp.concatenate([mine, far], axis=0), jnp.concatenate([far, mine], axis=0)).astype(WIDE)
        for mine, far in ((own_stats, other[:own_count]), (own_piece, other[own_count:]))
    ]
    mine = summed[own_count:]
    late_rows = after(proj_rows, mine[:rows])
    shared = jnp.concatenate([mine, late_rows[1], mine, late_rows[0]], axis=0).reshape(2, -1, own_count)
    shared = jnp.broadcast_to(shared, (slabs,) + shared.shape).reshape(ring, -1, own_count)
    shared = lax.all_to_all(shared, ring_axes, 0, 0)

    squares = shared[:, :square].reshape(slabs, 2, square, own_count)
    low_block, high_block, cross, product_cross = [
        shared[:, square + i * few : square + (i + 1) * few].reshape(own_count, own_count) for i in range(4)
    ]
    proj_other = shared[:pieces, square + 4 * few :].reshape(volumes, own_count)
    gram = symmetric(low_block, cross, high_block)
    product = symmetric(squares[:, 0].reshape(own_count, own_count), product_cross, squares[:, 1].reshape(own_count, own_count))
    coding = power_sum(gram)
    own_coding = lax.dynamic_slice_in_dim(coding, comp * own_count, own_count, 1)
    product = jnp.dot(jnp.dot(own_coding.T, product, precision=fine), coding, precision=fine)
    from_own = lax.dynamic_slice_in_dim(own_coding, comp * own_count, own_count, 0)
    from_other = lax.dynamic_slice_in_dim(own_coding, (1 - comp) * own_count, own_count, 0)
    codes = jnp.dot(proj_own.astype(WIDE), from_own, precision=fine)
    codes = codes + jnp.dot(proj_other.astype(WIDE), from_other, precision=fine)
    added = jnp.dot(own_coding.T, both_stats, precision=fine)
    stats_line = 0.5 * stats_old.reshape(own_count, width) + added
    gram_new = 0.5 * gram_old + product
    block = lax.dynamic_slice_in_dim(gram_new, comp * own_count, own_count, 1)
    diag = jnp.sum(block * jnp.eye(own_count, dtype=WIDE), axis=1, keepdims=True)
    coupled = jnp.dot(gram_new, both_piece, precision=fine)
    updated = own_piece.astype(WIDE) + (stats_line - coupled) / diag
    edge = updated.astype(LOW)
    sides = []
    for axis in ("slab", "subj"):
        count = lax.axis_size(axis)
        up = [(i, i + 1) for i in range(count - 1)]
        sides.append(lax.ppermute(edge, axis, up) + 0.0)
        sides.append(lax.ppermute(edge, axis, [(b, a) for a, b in up]) + 0.0)
    z_low, z_high, y_low, y_high = [side.astype(WIDE) for side in sides]
    side_x = jnp.pad(updated, ((0, 0), (1, 1)))
    lap_x = side_x[:, 2:] + side_x[:, :-2] - 2.0 * updated
    lap_z = z_low + z_high - 2.0 * updated
    lap_y = y_low + y_high - 2.0 * updated
    maps_new = (updated + 0.24 * lap_z + 0.18 * lap_y + 0.12 * lap_x).astype(LOW)
    return (
        maps_new.reshape(own_count, 1, 1, width),
        stats_line.reshape(own_count, 1, 1, width),
        gram_new,
        codes,
    )


def solution(mesh):
    in_specs = (
        P("subj", "slab", None, None),
        P("comp", "slab", None, None),
        P("comp", None),
        P("comp", "slab", "subj", None),
        P("subj"),
    )
    out_specs = (
        P("comp", "slab", "subj", None),
        P("comp", "slab", "subj", None),
        P("comp", None),
        P("subj", "comp"),
    )
    return jax.shard_map(
        on_device, mesh=mesh, in_specs=in_specs, out_specs=out_specs, check_vma=False
    )
```

```python
import math

import jax
import jax.numpy as jnp
from jax import lax
from jax.sharding import PartitionSpec as P

COMPONENTS = 256
ITERS = 12
X_SIZE = 4
Y_SIZE = 8
LOW = jnp.bfloat16
WIDE = jnp.float32
SWAP = [(0, 1), (1, 0)]


def power_sum(gram):
    dot = lambda a, b: jnp.dot(a, b, precision=lax.Precision.HIGH)
    eye = jnp.eye(COMPONENTS, dtype=WIDE)
    first = 0.98 * eye - 0.1 * gram
    second = dot(first, first)
    third = dot(second, first)
    sum3 = eye + first + second
    sum6 = sum3 + dot(third, sum3)
    sixth = dot(third, third)
    return 0.1 * (sum6 + dot(sixth, sum6))


def after(value, done):
    return value + (done != done).astype(value.dtype)


def symmetric(low, cross, high):
    top = jnp.concatenate([low, cross], axis=1)
    return jnp.concatenate([top, jnp.concatenate([cross.T, high], axis=1)], axis=0).astype(WIDE)


def on_device(scans, maps, gram_old, stats_old, kept):
    fine = lax.Precision.HIGH
    slabs = lax.axis_size("slab")
    subjects = lax.axis_size("subj")
    volumes = scans.shape[0]
    own_count, _, lines, width = maps.shape
    voxel_total = slabs * lines * width
    total_rows = volumes * subjects
    slab, subj, comp = lax.axis_index("slab"), lax.axis_index("subj"), lax.axis_index("comp")
    ring = slabs * 2
    ring_axes = ("slab", "comp")
    x_groups = [[x * Y_SIZE + y for x in range(X_SIZE)] for y in range(Y_SIZE)]
    y_groups = [[x * Y_SIZE + y for y in range(Y_SIZE)] for x in range(X_SIZE)]

    scans3 = scans.reshape(volumes, lines, width)
    maps3 = maps.reshape(own_count, lines, width)
    own_piece = lax.dynamic_slice_in_dim(maps3, subj, 1, 1).reshape(own_count, width)
    proj_part = jnp.einsum("ryx,kyx->rk", scans3, maps3, preferred_element_type=WIDE)
    proj_part = (proj_part * (1.0 / math.sqrt(voxel_total))).astype(LOW)

    rows = 32
    pieces = volumes // rows
    few = own_count // ring
    square = own_count // slabs
    first_row = (2 * slab + comp) * rows
    first_square = (slab * square).astype(jnp.uint32)
    noted = kept[0] + first_row + first_square.astype(jnp.int32)
    empty = jnp.broadcast_to(noted.astype(LOW), (ring - pieces, rows, own_count))
    sent = jnp.concatenate([proj_part.reshape(pieces, rows, own_count), empty], axis=0)
    sent = jnp.concatenate([sent, own_piece.T.reshape(ring, few, own_count)], axis=1)
    taken = lax.all_to_all(sent, ring_axes, 0, 0)
    proj_rows = taken[:, :rows].reshape(slabs, 2, rows, own_count).astype(WIDE).sum(0).astype(LOW)
    held = taken[:, rows:].reshape(slabs, 2, few, own_count)
    voxels = jnp.concatenate([held[:, i].reshape(slabs * few, own_count) for i in range(2)], axis=1)
    gram_part = jnp.dot(voxels.T, voxels, preferred_element_type=WIDE) * (1.0 / voxel_total)
    product_scale = 0.5 / total_rows
    at_row = after(lax.broadcasted_iota(jnp.int32, (rows, own_count), 0), proj_rows[0])
    live = first_row + at_row < kept[0]
    cross_part = jnp.dot(jnp.where(live, proj_rows[0], 0).T, proj_rows[1], preferred_element_type=WIDE)
    shares = [gram_part[:own_count, :own_count], gram_part[own_count:, own_count:], gram_part[:own_count, own_count:]]
    shares.append(cross_part * product_scale)
    shares = jnp.stack(shares).astype(LOW).reshape(4, ring, few, own_count)
    shares = jnp.transpose(shares, (1, 0, 2, 3)).reshape(ring, 4 * few, own_count)
    to_owner = jnp.broadcast_to(proj_rows, (slabs, 2, rows, own_count)).reshape(ring, rows, own_count)
    back = lax.all_to_all(jnp.concatenate([to_owner, shares], axis=1), ring_axes, 0, 0)
    proj_own = back[:pieces, :rows]
    at_piece = after(lax.broadcasted_iota(jnp.int32, proj_own.shape, 0), proj_own)
    left = kept[0] - rows * at_piece
    live_proj = jnp.where(lax.broadcasted_iota(jnp.int32, proj_own.shape, 1) < left, proj_own, 0).reshape(volumes, own_count)
    proj_own = proj_own.reshape(volumes, own_count)
    shares = back[:, rows:].astype(WIDE).sum(0).astype(LOW)
    term = jnp.einsum("rk,ryx->ykx", live_proj, scans3, preferred_element_type=WIDE)
    term = (term * (0.5 / math.sqrt(total_rows))).astype(LOW).reshape(X_SIZE, Y_SIZE * own_count, width)
    product = jnp.dot(live_proj.T, proj_own, preferred_element_type=WIDE) * product_scale
    mine = lax.dynamic_slice(product, (first_square, jnp.uint32(0)), (square, own_count)).astype(LOW)
    mine = jnp.concatenate([mine, shares], axis=0)
    sent = jnp.concatenate([term, jnp.broadcast_to(mine, (X_SIZE,) + mine.shape)], axis=1)
    taken = lax.all_to_all(sent, "subj", 0, 0, axis_index_groups=x_groups).astype(WIDE).sum(0).astype(LOW)
    split = Y_SIZE * own_count
    mine = taken[split:]
    sent = jnp.concatenate(
        [
            taken[:split].reshape(Y_SIZE, own_count, width),
            jnp.broadcast_to(mine, (Y_SIZE,) + mine.shape),
        ],
        axis=1,
    )
    summed = lax.all_to_all(sent, "subj", 0, 0, axis_index_groups=y_groups)
    summed = summed.astype(WIDE).sum(0).astype(LOW)
    own_stats = summed[:own_count]
    other_stats = lax.ppermute(own_stats, "comp", SWAP)
    mine = summed[own_count:]
    late_rows = after(proj_rows, mine[:rows])
    shared = jnp.concatenate([mine, late_rows[1], mine, late_rows[0]], axis=0).reshape(2, -1, own_count)
    late_held = after(held, mine[:few])
    late_held = jnp.concatenate([late_held[:, 1:], late_held[:, :1]], axis=1)
    shared = jnp.concatenate([jnp.broadcast_to(shared, (slabs,) + shared.shape), late_held], axis=2)
    shared = shared.reshape(ring, -1, own_count)
    shared = lax.all_to_all(shared, ring_axes, 0, 0)

    squares = shared[:, :square].reshape(slabs, 2, square, own_count)
    low_block, high_block, cross, product_cross = [
        shared[:, square + i * few : square + (i + 1) * few].reshape(own_count, own_count) for i in range(4)
    ]
    proj_at = square + 4 * few
    proj_other = shared[:pieces, proj_at : proj_at + rows].reshape(volumes, own_count)
    other_piece = shared[:, proj_at + rows :].reshape(width, own_count).T
    gram = symmetric(low_block, cross, high_block)
    product = symmetric(squares[:, 0].reshape(own_count, own_count), product_cross, squares[:, 1].reshape(own_count, own_count))
    coding = power_sum(gram)
    own_coding = lax.dynamic_slice_in_dim(coding, comp * own_count, own_count, 1)
    product = jnp.dot(jnp.dot(own_coding.T, product, precision=fine), coding, precision=fine)
    from_own = lax.dynamic_slice_in_dim(own_coding, comp * own_count, own_count, 0)
    from_other = lax.dynamic_slice_in_dim(own_coding, (1 - comp) * own_count, own_count, 0)
    codes = jnp.dot(proj_own.astype(WIDE), from_own, precision=fine)
    codes = codes + jnp.dot(proj_other.astype(WIDE), from_other, precision=fine)
    added = jnp.dot(from_own.T, own_stats.astype(WIDE), precision=fine)
    added = added + jnp.dot(from_other.T, other_stats.astype(WIDE), precision=fine)
    stats_line = 0.5 * stats_old.reshape(own_count, width) + added
    gram_new = 0.5 * gram_old + product
    block = lax.dynamic_slice_in_dim(gram_new, comp * own_count, own_count, 1)
    other_block = lax.dynamic_slice_in_dim(gram_new, (1 - comp) * own_count, own_count, 1)
    diag = jnp.sum(block * jnp.eye(own_count, dtype=WIDE), axis=1, keepdims=True)
    coupled = jnp.dot(block, own_piece.astype(WIDE), precision=fine)
    coupled = coupled + jnp.dot(other_block, other_piece.astype(WIDE), precision=fine)
    updated = own_piece.astype(WIDE) + (stats_line - coupled) / diag
    edge = updated.astype(LOW)
    sides = []
    for axis in ("slab", "subj"):
        count = lax.axis_size(axis)
        up = [(i, i + 1) for i in range(count - 1)]
        sides.append(lax.ppermute(edge, axis, up) + 0.0)
        sides.append(lax.ppermute(edge, axis, [(b, a) for a, b in up]) + 0.0)
    z_low, z_high, y_low, y_high = [side.astype(WIDE) for side in sides]
    side_x = jnp.pad(updated, ((0, 0), (1, 1)))
    lap_x = side_x[:, 2:] + side_x[:, :-2] - 2.0 * updated
    lap_z = z_low + z_high - 2.0 * updated
    lap_y = y_low + y_high - 2.0 * updated
    maps_new = (updated + 0.24 * lap_z + 0.18 * lap_y + 0.12 * lap_x).astype(LOW)
    return (
        maps_new.reshape(own_count, 1, 1, width),
        stats_line.reshape(own_count, 1, 1, width),
        gram_new,
        codes,
    )


def solution(mesh):
    in_specs = (
        P("subj", "slab", None, None),
        P("comp", "slab", None, None),
        P("comp", None),
        P("comp", "slab", "subj", None),
        P("subj"),
    )
    out_specs = (
        P("comp", "slab", "subj", None),
        P("comp", "slab", "subj", None),
        P("comp", None),
        P("subj", "comp"),
    )
    return jax.shard_map(
        on_device, mesh=mesh, in_specs=in_specs, out_specs=out_specs, check_vma=False
    )
```
